32 devices in a mesh: dp: 2 (over x), hs: 4 (over z), blk: 4 (over y, core).
Axes of the slice: x: 2, y: 2, z: 4, core: 2. Of those that a mesh axis runs over, the one named last changes fastest.
Arguments:
- tokens: bfloat16 [6144, 2048], P(('dp', 'hs', 'blk')), may hold values from -6 to 6
- block_order: int32 [2, 16], P('dp'), may hold values from 0 to 15, each once within a row
- gain_attn: bfloat16 [2048], P(('dp', 'hs', 'blk')), may hold values from 0.5 to 1.5
- w_qkv: bfloat16 [2048, 6144], P(('dp', 'hs', 'blk')), may hold values from -0.125 to 0.125
- w_out: bfloat16 [2048, 2048], P(('dp', 'hs', 'blk')), may hold values from -4 to 4
- gain_mlp: bfloat16 [2048], P(('dp', 'hs', 'blk')), may hold values from 0.5 to 1.5
- w_gate_up: bfloat16 [2048, 16384], P(('dp', 'hs', 'blk')), may hold values from -0.125 to 0.125
- w_down: bfloat16 [2048, 8192], P(('dp', 'hs', 'blk')), may hold values from -0.0625 to 0.0625
- cotangent: bfloat16 [6144, 2048], P(('dp', 'hs', 'blk')), may hold values from -6 to 6
Outputs:
- layer_out: bfloat16 [6144, 2048], P(('dp', 'hs', 'blk'))
- grad_tokens: float32 [6144, 2048], P(('dp', 'hs', 'blk'))
- grad_gain_attn: float32 [2048], P(('dp', 'hs', 'blk'))
- grad_w_qkv: float32 [2048, 6144], P(('dp', 'hs', 'blk'))
- grad_w_out: float32 [2048, 2048], P(('dp', 'hs', 'blk'))
- grad_gain_mlp: float32 [2048], P(('dp', 'hs', 'blk'))
- grad_w_gate_up: float32 [2048, 16384], P(('dp', 'hs', 'blk'))
- grad_w_down: float32 [2048, 8192], P(('dp', 'hs', 'blk'))
The draws below stay inside these ranges and needn't reach their ends.
Inputs may be any that keep to these rules, and one draw needn't show every extreme that they name: Each row of block_order names every block number of a sequence exactly once.
All inputs are finite; a program needn't handle non-finite values.
Results may differ from the reference program's by a relative error of at most 0.015.
Values may be sent and summed in bfloat16 or wider, within the bound.
A program may use at most 832 MiB of HBM per device.

```python
import jax
import jax.numpy as jnp
from jax import lax

D = 2048
HEADS = 32
HEAD_DIM = 64
FF = 8192
TOK_DEV = 192
BLOCKS = 16
LENGTH = 3072
TOKENS = 6144
N_DP = 2


def steps_of(own_key, dims, cuts, low, high):
    level = 1.0
    for position, parts in cuts:
        heights = jax.random.uniform(jax.random.fold_in(jax.random.fold_in(own_key, 6), position), (parts,), jnp.float32, low / len(cuts), high / len(cuts))
        level = level * jnp.repeat(jnp.exp(heights), dims[position] // parts).reshape((-1,) + (1,) * (len(dims) - 1 - position))
    return level


def noise(own_key, shape, deviation, limit, pieces=(), kind=jnp.bfloat16):
    drawn = deviation * jax.random.normal(own_key, shape, jnp.float32)
    if pieces:
        drawn = drawn * steps_of(own_key, shape, pieces, -0.22, 0.18)
    return jnp.clip(drawn, -limit, limit).astype(kind)


def setup_inputs(seed: int = 0) -> dict:
    key_list = jax.random.split(jax.random.key(seed), 10)
    tokens = noise(key_list[0], (TOKENS, D), 1.0, 6.0, ((0, 32),))
    block_order = jax.vmap(lambda own: jax.random.permutation(own, BLOCKS))(jax.random.split(key_list[1], N_DP)).reshape((N_DP, BLOCKS)).astype(jnp.int32)
    gain_attn = jnp.clip(1.0 + 0.1 * jax.random.normal(key_list[2], (D,), jnp.float32), 0.5, 1.5).astype(jnp.bfloat16)
    w_qkv = noise(key_list[3], (D, 3 * D), D ** -0.5, 0.125, ((0, 32),))
    w_out = noise(key_list[4], (D, D), (max(D // (4 * TOK_DEV), 1)) ** -0.5, 4.0, ((0, 32),))
    gain_mlp = jnp.clip(1.0 + 0.1 * jax.random.normal(key_list[5], (D,), jnp.float32), 0.5, 1.5).astype(jnp.bfloat16)
    w_gate_up = noise(key_list[6], (D, 2 * FF), D ** -0.5, 0.125, ((0, 32),))
    w_down = noise(key_list[7], (D, FF), FF ** -0.5, 0.0625, ((0, 32),))
    cotangent = noise(key_list[8], (TOKENS, D), 1.0, 6.0, ((0, 32),))
    return {"tokens": tokens, "block_order": block_order, "gain_attn": gain_attn, "w_qkv": w_qkv, "w_out": w_out, "gain_mlp": gain_mlp, "w_gate_up": w_gate_up, "w_down": w_down, "cotangent": cotangent}


THETA = 130000.0
EPS = 1e-05
HIGH = lax.Precision.HIGHEST

@jax.custom_vjp
def low(v):
    return lax.optimization_barrier(v.astype(jnp.bfloat16)).astype(jnp.float32)

@jax.custom_vjp
def low_back(v):
    return v

def low_keep(v):
    return (low(v), None)

def low_pass(kept, grad):
    return (grad,)

def back_keep(v):
    return (v, None)

def back_low(kept, grad):
    return (low(grad),)
low.defvjp(low_keep, low_pass)
low_back.defvjp(back_keep, back_low)

def rotate(values, positions):
    half = values.shape[-1] // 2
    index = jnp.arange(half, dtype=jnp.float32)
    freq = jnp.power(jnp.float32(THETA), -2.0 * index / float(values.shape[-1]))
    angle = positions.astype(jnp.float32)[:, None] * freq[None, :]
    cosine = jnp.cos(angle)[:, None, :]
    sine = jnp.sin(angle)[:, None, :]
    first, second = (values[..., :half], values[..., half:])
    return jnp.concatenate([first * cosine - second * sine, second * cosine + first * sine], axis=-1)

def rms_scale(values, gain):
    return values * lax.rsqrt(lax.optimization_barrier(jnp.mean(values * values, axis=-1, keepdims=True)) + EPS) * gain

def attend(query, keys, values, query_pos, key_pos):
    scores = jnp.einsum('qhd,khd->hqk', query, keys, precision=HIGH) * HEAD_DIM ** (-0.5)
    scores = low_back(scores)
    allowed = (query_pos[:, None] >= key_pos[None, :])[None]
    masked = jnp.where(allowed, scores, -1e+30)
    top = lax.optimization_barrier(jnp.max(masked, axis=-1, keepdims=True))
    expo = jnp.where(allowed, jnp.exp(masked - top), 0.0)
    probs = expo / lax.optimization_barrier(jnp.sum(expo, axis=-1, keepdims=True))
    return jnp.einsum('hqk,khd->qhd', low(probs), values, precision=HIGH)

def forward(x, gain1, wqkv, wout, gain2, wgu, wdown, positions):
    rows = x.shape[0]
    xn1 = low(rms_scale(x, gain1))
    qkv = low_back(jnp.dot(xn1, wqkv, precision=HIGH))
    query = low(low_back(rotate(qkv[:, :D].reshape(rows, HEADS, HEAD_DIM), positions)))
    keys = low(low_back(rotate(qkv[:, D:2 * D].reshape(rows, HEADS, HEAD_DIM), positions)))
    values = low(qkv[:, 2 * D:].reshape(rows, HEADS, HEAD_DIM))
    block = min(512, rows)
    count = rows // block
    checked = jax.checkpoint(attend)
    ctx = lax.map(lambda item: checked(item[0], keys, values, item[1], positions), (query.reshape(count, block, HEADS, HEAD_DIM), positions.reshape(count, block)))
    ctx = low(low_back(ctx.reshape(rows, D)))
    y_mid = x + low_back(jnp.dot(ctx, wout, precision=HIGH))
    xn2 = low(rms_scale(y_mid, gain2))
    gate_up = low_back(jnp.dot(xn2, wgu, precision=HIGH))
    hidden = low(jax.nn.silu(gate_up[:, :FF]) * gate_up[:, FF:])
    return y_mid + jnp.dot(hidden, wdown.T, precision=HIGH)

def reference(tokens, block_order, gain_attn, w_qkv, w_out, gain_mlp, w_gate_up, w_down, cotangent):
    params = tuple((a.astype(jnp.float32) for a in (gain_attn, w_qkv, w_out, gain_mlp, w_gate_up, w_down)))
    inputs = tokens.astype(jnp.float32).reshape(N_DP, LENGTH, D)
    grads_in = cotangent.astype(jnp.float32).reshape(N_DP, LENGTH, D)
    offsets = jnp.arange(TOK_DEV, dtype=jnp.int32)

    def per_sequence(totals, item):
        x, cot, order = item
        positions = (order.astype(jnp.int32)[:, None] * TOK_DEV + offsets[None, :]).reshape(LENGTH).astype(jnp.int32)
        result, pull = jax.vjp(lambda xx, *pp: forward(xx, *pp, positions), x, *params)
        grads = pull(cot)
        totals = tuple((t + g for t, g in zip(totals, grads[1:])))
        return (totals, (result.astype(jnp.bfloat16), grads[0]))
    zeros = tuple((jnp.zeros_like(p) for p in params))
    totals, (results, dx) = lax.scan(per_sequence, zeros, (inputs, grads_in, block_order))
    return (results.reshape(N_DP * LENGTH, D), dx.reshape(N_DP * LENGTH, D), totals[0], totals[1], totals[2], totals[3], totals[4], totals[5])
```

```python
import functools

import jax
import jax.numpy as jnp
import numpy as np
from jax import lax
from jax.experimental import pallas as pl
from jax.experimental.pallas import tpu as pltpu
from jax.sharding import PartitionSpec as P

HEADS = 32
HEAD_DIM = 64
THETA = 130000.0
EPS = 1e-05
TP = ("hs", "blk")
ALL = ("dp", "hs", "blk")
VMEM_LIMIT = 56 * 1024 * 1024
EXP2_SCALE = HEAD_DIM**-0.5 * 1.4426950408889634

F32 = jnp.float32
BF16 = jnp.bfloat16


def dot_nn(a, b):
    return lax.dot_general(a, b, (((1,), (0,)), ((), ())), preferred_element_type=F32)


def dot_nt(a, b):
    return lax.dot_general(a, b, (((1,), (1,)), ((), ())), preferred_element_type=F32)


def dot_tn(a, b):
    return lax.dot_general(a, b, (((0,), (0,)), ((), ())), preferred_element_type=F32)


def rms_scale(values, gain):
    return values * lax.rsqrt(jnp.mean(values * values, axis=-1, keepdims=True) + EPS) * gain


def rope_tables(blocks, block):
    half = HEAD_DIM // 2
    lane = np.arange(2 * HEAD_DIM)
    index = jnp.asarray(lane % half, F32)
    sign = jnp.asarray(np.where(lane % HEAD_DIM < half, -1.0, 1.0), F32)
    freq = jnp.power(F32(THETA), -2.0 * index / float(HEAD_DIM))[None, :]
    base = (jnp.arange(blocks, dtype=jnp.int32) * block).astype(F32)[:, None] * freq
    step = jnp.arange(block, dtype=jnp.int32).astype(F32)[:, None] * freq
    cos, sin = jnp.cos(step), jnp.sin(step)
    return (
        jnp.stack([jnp.cos(base), jnp.sin(base)]),
        jnp.stack([cos, sin, cos * sign, sin * sign]),
    )


def rope_of_block(base_ref, step_ref, b):
    cos, sin = base_ref[0, pl.ds(b, 1), :], base_ref[1, pl.ds(b, 1), :]
    return (
        cos * step_ref[0] - sin * step_ref[1],
        sin * step_ref[2] + cos * step_ref[3],
    )


def swap_halves(x):
    half = HEAD_DIM // 2
    width = x.shape[1]
    lane = lax.broadcasted_iota(jnp.int32, x.shape, 1)
    return jnp.where(
        lax.rem(lane, HEAD_DIM) < half,
        pltpu.roll(x, width - half, 1),
        pltpu.roll(x, half, 1),
    )


MESH = pl.DeviceIdType.MESH
CHUNKS = 2


def position():
    z, b = lax.axis_index("hs"), lax.axis_index("blk")
    return z, b // 2, b % 2


def remote(src, dst, send, recv, **where):
    return pltpu.make_async_remote_copy(
        src_ref=src, dst_ref=dst, send_sem=send, recv_sem=recv, device_id=where, device_id_type=MESH
    )


def signal(sem, **where):
    pl.semaphore_signal(sem, inc=1, device_id=where, device_id_type=MESH)


def greet_neighbours(nz):
    z, y, c = position()
    barrier = pltpu.get_barrier_semaphore()
    signal(barrier, blk=y * 2 + 1 - c)
    signal(barrier, blk=(1 - y) * 2 + c)

    @pl.when(z > 0)
    def _():
        signal(barrier, hs=z - 1)

    @pl.when(z < nz - 1)
    def _():
        signal(barrier, hs=z + 1)

    count = 2 + jnp.where(z > 0, 1, 0) + jnp.where(z < nz - 1, 1, 0)
    pl.semaphore_wait(barrier, count)


def greet_all(nz, n_dp):
    z, y, c = position()
    peers = nz * 4
    me = z * 4 + y * 2 + c
    d = lax.axis_index("dp")
    barrier = pltpu.get_barrier_semaphore()

    @pl.loop(1, peers)
    def _(r):
        t = (me + r) % peers
        signal(barrier, hs=t // 4, blk=t % 4)

    @pl.loop(1, n_dp)
    def _(r):
        signal(barrier, dp=(d + r) % n_dp)

    pl.semaphore_wait(barrier, peers - 1 + n_dp - 1)


def by_distance(z, n, nz):
    near = jnp.minimum(z, nz - 1 - z)
    step = (n + 1) // 2
    both = jnp.where(n % 2 == 1, z - step, z + step)
    one = jnp.where(z < nz - 1 - z, n, nz - 1 - n)
    return jnp.where(n <= 2 * near, both, one)


def gather_sems(nz, chunks=CHUNKS):
    one, two = (nz, chunks), (nz, 2, chunks)
    return [pltpu.SemaphoreType.DMA(s) for s in (one, one, two, one, one, one, two)]


class Gather:
    def __init__(self, buf, sems, nz, lead=(), chunks=CHUNKS):
        self.buf, self.nz, self.lead, self.chunks = buf, nz, lead, chunks
        self.z, self.y, self.c = position()
        self.r_z, self.r_y, self.r_c, self.s_r, self.s_l, self.s_y, self.s_c = sems
        self.rows = buf.shape[-2] // chunks

    def part(self, zs, y, c, q):
        rows = pl.ds(pl.multiple_of(q * self.rows, self.rows), self.rows)
        return self.buf.at[(*self.lead, zs, y, c, rows, slice(None))]

    def right(self, zs, q):
        p = self.part(zs, self.y, self.c, q)
        return remote(p, p, self.s_r.at[zs, q], self.r_z.at[zs, q], hs=self.z + 1)

    def left(self, zs, q):
        p = self.part(zs, self.y, self.c, q)
        return remote(p, p, self.s_l.at[zs, q], self.r_z.at[zs, q], hs=self.z - 1)

    def across(self, zs, q):
        p = self.part(zs, self.y, self.c, q)
        return remote(
            p, p, self.s_y.at[zs, q], self.r_y.at[zs, q], blk=(1 - self.y) * 2 + self.c
        )

    def sibling(self, zs, y, q):
        p = self.part(zs, y, self.c, q)
        return remote(
            p, p, self.s_c.at[zs, y, q], self.r_c.at[zs, y, q], blk=self.y * 2 + 1 - self.c
        )

    def goes_right(self, zs):
        return jnp.logical_and(zs <= self.z, self.z < self.nz - 1)

    def goes_left(self, zs):
        return jnp.logical_and(zs >= self.z, self.z > 0)

    def row_part(self, n, q):
        zs = by_distance(self.z, n, self.nz)

        @pl.when(n > 0)
        def _():
            p = self.part(zs, self.y, self.c, q)
            remote(
                p, p, self.s_y.at[zs, q], self.r_z.at[zs, q], blk=self.y * 2 + 1 - self.c
            ).wait_recv()

        @pl.when(self.goes_right(zs))
        def _():
            self.right(zs, q).start()

        @pl.when(self.goes_left(zs))
        def _():
            self.left(zs, q).start()

        self.across(zs, q).start()
        self.sibling(zs, self.y, q).start()

    def cross_part(self, n, q):
        zs = by_distance(self.z, n, self.nz)
        p = self.part(zs, 1 - self.y, self.c, q)
        remote(
            p, p, self.s_y.at[zs, q], self.r_y.at[zs, q], blk=(1 - self.y) * 2 + self.c
        ).wait_recv()
        self.sibling(zs, 1 - self.y, q).start()

    def row_step(self, n):
        for q in range(self.chunks):
            self.row_part(n, q)

    def cross_step(self, n):
        for q in range(self.chunks):
            self.cross_part(n, q)

    def chunk_step(self, e):
        @pl.when(e < self.nz * self.chunks)
        def _():
            self.row_part(e // self.chunks, e % self.chunks)

        self.cross_part((e - self.chunks) // self.chunks, e % self.chunks)

    def ready(self, zs, y):
        for q in range(self.chunks):
            p = self.part(zs, y, 1 - self.c, q)
            remote(
                p, p, self.s_c.at[zs, y, q], self.r_c.at[zs, y, q], blk=self.y * 2 + 1 - self.c
            ).wait_recv()

    def drain(self):
        @pl.loop(0, self.nz)
        def _(zs):
            for q in range(self.chunks):

                @pl.when(self.goes_right(zs))
                def _():
                    self.right(zs, q).wait_send()

                @pl.when(self.goes_left(zs))
                def _():
                    self.left(zs, q).wait_send()

                self.across(zs, q).wait_send()
                self.sibling(zs, 0, q).wait_send()
                self.sibling(zs, 1, q).wait_send()


class DpGather:
    def __init__(self, buf, sems, nz, n_dp):
        self.d, self.n_dp, self.nz, self.buf = lax.axis_index("dp"), n_dp, nz, buf
        self.s_x, self.r_x, self.s_f, self.r_f = sems[:4]
        self.plane = Gather(buf, sems[4:], nz, (self.d,), 1)
        self.z, self.y, self.c = position()

    def to_dp(self, zs, y, r):
        p = self.buf.at[self.d, zs, y, self.c]
        sems = self.s_x.at[zs, y, r], self.r_x.at[zs, y, r]
        return remote(p, p, *sems, dp=(self.d + r) % self.n_dp)

    def relay(self, zs, y, c, r, sems):
        p = self.buf.at[(self.d + self.n_dp - r) % self.n_dp, zs, y, c]
        sems = (sem.at[zs, y, r] for sem in sems)
        return remote(p, p, *sems, blk=self.y * 2 + 1 - self.c)

    def row_step(self, n):
        self.plane.row_step(n)
        self.send_on(by_distance(self.z, n, self.nz), self.y)

    def cross_step(self, n):
        self.plane.cross_step(n)
        self.send_on(by_distance(self.z, n, self.nz), 1 - self.y)

    def send_on(self, zs, y):
        @pl.loop(1, self.n_dp)
        def _(r):
            self.to_dp(zs, y, r).start()

    def each(self, act):
        @pl.loop(0, self.nz)
        def _(n):
            zs = by_distance(self.z, n, self.nz)
            for y in (self.y, 1 - self.y):

                @pl.loop(1, self.n_dp)
                def _(r):
                    act(zs, y, r)

    def finish(self):
        def pass_on(zs, y, r):
            self.relay(zs, y, self.c, r, (self.s_x, self.r_x)).wait_recv()
            self.relay(zs, y, self.c, r, (self.s_f, self.r_f)).start()

        def end(zs, y, r):
            self.relay(zs, y, 1 - self.c, r, (self.s_f, self.r_f)).wait_recv()
            self.relay(zs, y, self.c, r, (self.s_f, self.r_f)).wait_send()
            self.to_dp(zs, y, r).wait_send()

        self.each(pass_on)

        @pl.loop(0, self.nz)
        def _(zs):
            self.plane.ready(zs, 0)
            self.plane.ready(zs, 1)

        self.each(end)
        self.plane.drain()


def dp_gather_sems(nz, n_dp):
    return [pltpu.SemaphoreType.DMA((nz, 2, n_dp)) for _ in range(4)] + gather_sems(nz, 1)


def scatter_sems(nz):
    return [pltpu.SemaphoreType.DMA((nz * CHUNKS,)) for _ in range(7)]


def scatter_buffers(nz, rows, width):
    two, one = pltpu.VMEM((nz, 2, rows, width), BF16), pltpu.VMEM((nz, rows, width), BF16)
    return [two, two, one, pltpu.VMEM((nz + 1, rows, width), BF16)]


class Scatter:
    def __init__(self, theirs, bufs, sems, nz):
        self.theirs, self.nz = theirs, nz
        self.mine, self.rc, self.ry, self.rz = bufs
        self.s_c, self.r_c, self.s_y, self.r_y, self.s_z, self.r_l, self.r_r = sems
        self.z, self.y, self.c = position()
        self.rows = self.mine.shape[2] // CHUNKS
        self.units = nz * CHUNKS
        self.steps = self.units + nz + 1

    def place(self, k):
        r = k % (2 * CHUNKS)
        pair = k // (2 * CHUNKS)
        return jnp.where(r % 2 == 0, self.nz - 1 - pair, pair), r // 2

    def unit(self, k):
        zs, q = self.place(k)
        return zs, pl.ds(q * self.rows, self.rows)

    def to_sibling(self, k):
        zs, part = self.unit(k)
        return remote(
            self.theirs(zs, part), self.rc.at[zs, :, part, :], self.s_c.at[k], self.r_c.at[k],
            blk=self.y * 2 + 1 - self.c,
        )

    def across(self, k):
        zs, part = self.unit(k)
        return remote(
            self.mine.at[zs, 1 - self.y, part, :], self.ry.at[zs, part, :],
            self.s_y.at[k], self.r_y.at[k], blk=(1 - self.y) * 2 + self.c,
        )

    def right(self, k):
        zs, part = self.unit(k)
        return remote(
            self.mine.at[zs, self.y, part, :], self.rz.at[zs, part, :],
            self.s_z.at[k], self.r_l.at[k], hs=self.z + 1,
        )

    def left(self, k):
        zs, part = self.unit(k)
        place = jnp.where(zs == self.z - 1, self.nz, zs)
        return remote(
            self.mine.at[zs, self.y, part, :], self.rz.at[place, part, :],
            self.s_z.at[k], self.r_r.at[k], hs=self.z - 1,
        )

    def take(self, buf, sem, k, place=None):
        zs, part = self.unit(k)
        place = zs if place is None else place
        p = buf.at[place, part, :]
        remote(p, p, self.s_z.at[k], sem.at[k], blk=self.y * 2 + 1 - self.c).wait_recv()
        return buf[place, part, :].astype(F32)

    def add(self, k, row, other):
        zs, part = self.unit(k)
        self.mine[zs, row, part, :] = (self.mine[zs, row, part, :].astype(F32) + other).astype(
            BF16
        )

    def chip_sum(self, k):
        zs, part = self.unit(k)
        self.to_sibling(k).wait_recv()
        self.add(k, 1 - self.y, self.rc[zs, 1 - self.y, part, :].astype(F32))
        self.across(k).start()
        self.add(k, self.y, self.rc[zs, self.y, part, :].astype(F32))

    def row_sum(self, k):
        self.add(k, self.y, self.take(self.ry, self.r_y, k))

    def pass_on(self, k, buf, sem, start, first):
        @pl.when(jnp.logical_not(first))
        def _():
            self.add(k, self.y, self.take(buf, sem, k))

        start(k).start()

    def finish(self, k, out_ref):
        zs, part = self.unit(k)
        out_ref[part, :] = self.mine[zs, self.y, part, :].astype(F32)

        @pl.when(self.z > 0)
        def _():
            out_ref[part, :] += self.take(self.rz, self.r_l, k)

        @pl.when(self.z < self.nz - 1)
        def _():
            out_ref[part, :] += self.take(self.rz, self.r_r, k, self.nz)

    def step(self, k, out_ref):
        @pl.when(k < self.units)
        def _():
            self.chip_sum(k)

        self.later(k, out_ref)

    def later(self, k, out_ref):
        z, nz = self.z, self.nz

        def valid(m):
            return jnp.logical_and(m >= 0, m < self.units)

        @pl.when(valid(k - 1))
        def _():
            self.row_sum(k - 1)

        m = k - 1 - z

        @pl.when(jnp.logical_and(valid(m), self.unit(m)[0] > z))
        def _():
            self.pass_on(m, self.rz, self.r_l, self.right, z == 0)

        w = k - 1 - (nz - 1 - z)

        @pl.when(jnp.logical_and(valid(w), self.unit(w)[0] < z))
        def _():
            self.pass_on(w, self.rz, self.r_r, self.left, z == nz - 1)

        f = k - 1 - jnp.maximum(z, nz - 1 - z)

        @pl.when(jnp.logical_and(valid(f), self.unit(f)[0] == z))
        def _():
            self.finish(f, out_ref)

    def drain(self):
        @pl.loop(0, self.units)
        def _(k):
            self.to_sibling(k).wait_send()
            self.across(k).wait_send()

            @pl.when(self.unit(k)[0] > self.z)
            def _():
                self.right(k).wait_send()

            @pl.when(self.unit(k)[0] < self.z)
            def _():
                self.left(k).wait_send()


def exchange_sems(nz):
    dma = pltpu.SemaphoreType.DMA
    return [dma((nz * 4,)), dma((nz * 4,)), dma]


class Exchange:
    def __init__(self, src, dst, sems, nz):
        self.src, self.dst = src, dst
        self.send, self.recv, self.own = sems
        self.peers = nz * 4
        z, y, c = position()
        self.me = z * 4 + y * 2 + c

    def copy(self, r):
        t = (self.me + r) % self.peers
        return remote(
            self.src(t), self.dst(self.me), self.send.at[r], self.recv.at[r],
            hs=t // 4, blk=t % 4,
        )

    def arrival(self, r):
        t = (self.me + self.peers - r) % self.peers
        p = self.dst(t)
        return remote(p, p, self.send.at[r], self.recv.at[r], hs=t // 4, blk=t % 4)

    def keep(self):
        return pltpu.make_async_copy(self.src(self.me), self.dst(self.me), self.own)

    def start(self):
        self.keep().start()

        @pl.loop(1, self.peers)
        def _(r):
            self.copy(r).start()

    def arrive(self):
        self.keep().wait()

        @pl.loop(1, self.peers)
        def _(r):
            self.arrival(r).wait_recv()

    def drain(self):
        @pl.loop(1, self.peers)
        def _(r):
            self.copy(r).wait_send()


def attn_fwd_kernel(
    nz, n_dp, block, tile, slot_ref, order_ref, qkv_ref, base_ref, step_ref, cot_ref, wm_ref,
    q_out, k_out, v_out, ctxt_out, lse_out, ctx_out, cot_all, wm_in,
    qm, vt, ctx_sorted, ctx_blocks, ctx_slots, g, own_sem, o_cot, s_x, r_x, *sems,
):
    gather = Gather(g, sems[3:], nz)
    z, y, c = gather.z, gather.y, gather.c
    d = lax.axis_index("dp")
    own = pltpu.make_async_copy(cot_ref, g.at[z, y, c], own_sem)
    own.start()

    def x_copy(r):
        return remote(
            wm_ref, wm_in.at[r - 1], s_x.at[r], r_x.at[r], dp=(d + r) % n_dp
        )

    def cot_copy(zs, yy):
        return pltpu.make_async_copy(g.at[zs, yy], cot_all.at[zs, yy], o_cot.at[zs, yy])
    moves = Exchange(
        lambda t: ctx_slots.at[t],
        lambda t: ctx_out.at[:, pl.ds(pl.multiple_of(t * 2 * HEAD_DIM, 128), 2 * HEAD_DIM)],
        sems[:3],
        nz,
    )
    greet_all(nz, n_dp)
    own.wait()
    gather.row_step(0)

    @pl.loop(1, n_dp)
    def _(r):
        x_copy(r).start()

    length = q_out.shape[0]
    width = 2 * HEAD_DIM
    n_blocks = length // block
    n_tiles = length // tile

    @pl.loop(0, n_blocks)
    def _(b):
        dst = pl.ds(pl.multiple_of(b * block, block), block)
        cos, sin = rope_of_block(base_ref, step_ref, b)
        qkv = qkv_ref[slot_ref[b]]
        q = qkv[:, 0:width]
        k = qkv[:, width : 2 * width]
        v = qkv[:, 2 * width : 3 * width]
        q = (q * cos + swap_halves(q) * sin).astype(BF16)
        k = (k * cos + swap_halves(k) * sin).astype(BF16)
        q_out[dst, :] = q
        k_out[dst, :] = k
        v_out[dst, :] = v.astype(BF16)
        low = lax.broadcasted_iota(jnp.int32, q.shape, 1) < HEAD_DIM
        zero = jnp.zeros_like(q)
        qm[0, dst, :] = jnp.where(low, q, zero)
        qm[1, dst, :] = jnp.where(low, zero, q)

    @pl.loop(0, n_tiles)
    def _(t):
        rows = pl.ds(pl.multiple_of(t * tile, tile), tile)
        both = v_out[rows, :].astype(F32).T.astype(BF16)
        for h in range(2):
            vt[h, 0:HEAD_DIM, rows] = both[h * HEAD_DIM : (h + 1) * HEAD_DIM, :]
            vt[h, HEAD_DIM:, rows] = jnp.ones((16, tile), BF16)

    diag = lax.broadcasted_iota(jnp.int32, (tile, tile), 0) <= lax.broadcasted_iota(
        jnp.int32, (tile, tile), 1
    )

    @pl.loop(0, n_tiles)
    def _(i):
        rows_q = pl.ds(pl.multiple_of(i * tile, tile), tile)
        queries = [qm[0, rows_q, :], qm[1, rows_q, :]]

        def step(j, carry, masked):
            rows_k = pl.ds(pl.multiple_of(j * tile, tile), tile)
            keys = k_out[rows_k, :]
            new = []
            for h in range(2):
                top, acc = carry[h]
                s = dot_nt(keys, queries[h]) * EXP2_SCALE
                if masked:
                    s = jnp.where(diag, s, -1e30)
                new_top = jnp.maximum(top, jnp.max(s, axis=0, keepdims=True))
                p = jnp.exp2(s - new_top).astype(BF16)
                acc = acc * jnp.exp2(top - new_top) + dot_nn(vt[h, :, rows_k], p)
                new.append((new_top, acc))
            return tuple(new)

        start = tuple(
            (jnp.full((1, tile), -1e30, F32), jnp.zeros((HEAD_DIM + 16, tile), F32))
            for _ in range(2)
        )
        carry = lax.fori_loop(0, i, lambda j, c: step(j, c, False), start)
        carry = step(i, carry, True)
        outs = []
        for h in range(2):
            top, acc = carry[h]
            total = acc[HEAD_DIM : HEAD_DIM + 1, :]
            outs.append(acc[0:HEAD_DIM, :] / total)
            lse_out[h : h + 1, rows_q] = top + jnp.log2(total)
        both = jnp.concatenate(outs, axis=0)
        ctxt_out[:, rows_q] = both
        ctx_sorted[rows_q, :] = both.T.astype(BF16)

        for e, at in ((2, 5), (3, 3), (4, 2), (5, 1)):

            @pl.when(i == n_tiles - at)
            def _():
                gather.chunk_step(e)

    @pl.loop(0, n_blocks)
    def _(b):
        ctx_blocks[b] = ctx_sorted[pl.ds(pl.multiple_of(b * block, block), block), :]

    @pl.loop(0, n_blocks)
    def _(t):
        ctx_slots[t] = ctx_blocks[order_ref[t]]

    moves.start()

    @pl.loop(6, nz * CHUNKS + CHUNKS)
    def _(e):
        gather.chunk_step(e)

    @pl.loop(0, nz)
    def _(n):
        zs = by_distance(z, n, nz)
        for yy in (y, 1 - y):
            gather.ready(zs, yy)
            cot_copy(zs, yy).start()

    moves.arrive()
    moves.drain()
    gather.drain()

    @pl.loop(0, nz)
    def _(zs):
        for yy in range(2):
            cot_copy(zs, yy).wait()

    @pl.loop(1, n_dp)
    def _(r):
        x_copy(r).wait()


def attn_fwd(slot_of_block, order, qkv, base, step, cot, wm, nz, n_dp, tile):
    length = qkv.shape[0]
    width = 2 * HEAD_DIM
    block, wide = cot.shape
    whole = pl.BlockSpec(memory_space=pltpu.VMEM)
    smem = pl.BlockSpec(memory_space=pltpu.SMEM)
    any_spec = pl.BlockSpec(memory_space=pl.ANY)
    *rest, cot_all, wm_in = pl.pallas_call(
        functools.partial(attn_fwd_kernel, nz, n_dp, block, tile),
        in_specs=[smem, smem, whole, whole, whole, any_spec, any_spec],
        out_specs=[whole] * 5 + [any_spec] * 3,
        out_shape=[
            jax.ShapeDtypeStruct((length, width), BF16),
            jax.ShapeDtypeStruct((length, width), BF16),
            jax.ShapeDtypeStruct((length, width), BF16),
            jax.ShapeDtypeStruct((width, length), F32),
            jax.ShapeDtypeStruct((2, length), F32),
            jax.ShapeDtypeStruct((block, wide), BF16),
            jax.ShapeDtypeStruct((nz, 2, 2, block, wide), BF16),
            jax.ShapeDtypeStruct((max(n_dp - 1, 1),) + wm.shape, BF16),
        ],
        scratch_shapes=[
            pltpu.VMEM((2, length, width), BF16),
            pltpu.VMEM((2, HEAD_DIM + 16, length), BF16),
            pltpu.VMEM((length, width), BF16),
            pltpu.VMEM((length // block, block, width), BF16),
            pltpu.VMEM((length // block, block, width), BF16),
            pltpu.VMEM((nz, 2, 2, block, wide), BF16),
            pltpu.SemaphoreType.DMA,
            pltpu.SemaphoreType.DMA((nz, 2)),
            pltpu.SemaphoreType.DMA((n_dp,)),
            pltpu.SemaphoreType.DMA((n_dp,)),
        ]
        + exchange_sems(nz)
        + gather_sems(nz),
        compiler_params=pltpu.CompilerParams(
            vmem_limit_bytes=VMEM_LIMIT, collective_id=5, has_side_effects=True
        ),
        cost_estimate=pl.CostEstimate(
            flops=20 * length * length * HEAD_DIM,
            bytes_accessed=30 * length * wide,
            transcendentals=length * length,
        ),
        name="attn_fwd",
    )(slot_of_block, order, qkv.reshape(length // block, block, -1), base, step, cot, wm)
    return *rest, cot_all.reshape(length, wide), wm_in


def attn_bwd_kernel(
    nz, n_dp, block, tile,
    slot_ref, order_ref, q_ref, k_ref, v_ref, dctx_ref, ctxt_ref, lse_ref, base_ref, step_ref, p_ref, go_ref, xn_ref,
    out_ref, sum_ref, go_in, gq_ref,
    qm, dom, do_slots, do_sorted, kt, delta, dqt, dk_buf, dv_buf, d_blocks, acc, x_buf, l_x, l_m, s_x, r_x, *rest,
):
    bufs, sems = rest[:4], rest[4:]
    sc = Scatter(lambda zs, part: p_ref.at[zs, :, 1 - sc.c, part, :], bufs, sems[3:], nz)
    moves = Exchange(
        lambda t: dctx_ref.at[:, pl.ds(pl.multiple_of(t * 2 * HEAD_DIM, 128), 2 * HEAD_DIM)],
        lambda t: do_slots.at[t],
        sems[:3],
        nz,
    )

    def load(k):
        zs, part = sc.unit(k)
        return pltpu.make_async_copy(
            p_ref.at[zs, :, sc.c, part, :], bufs[0].at[zs, :, part, :], l_m.at[k]
        )

    d = lax.axis_index("dp")

    def x_copy(r):
        t = (d + r) % n_dp
        return remote(go_ref.at[t], go_in.at[r], s_x.at[r], r_x.at[r], dp=t)

    greet_all(nz, n_dp)
    moves.start()

    @pl.loop(1, n_dp)
    def _(r):
        x_copy(r).start()

    @pl.loop(0, sc.units)
    def _(k):
        sc.to_sibling(k).start()
        load(k).start()

    @pl.loop(0, sc.units)
    def _(k):
        load(k).wait()
        sc.chip_sum(k)

    moves.arrive()
    length = q_ref.shape[0]
    width = 2 * HEAD_DIM
    n_blocks = length // block
    n_tiles = length // tile
    scale = HEAD_DIM**-0.5

    @pl.loop(0, n_blocks)
    def _(b):
        dst = pl.ds(pl.multiple_of(b * block, block), block)
        do_sorted[dst, :] = do_slots[slot_ref[b]]

    @pl.loop(0, n_tiles)
    def _(t):
        rows = pl.ds(pl.multiple_of(t * tile, tile), tile)
        low = lax.broadcasted_iota(jnp.int32, (tile, width), 1) < HEAD_DIM
        q = q_ref[rows, :]
        do = do_sorted[rows, :]
        zero = jnp.zeros_like(q)
        qm[0, rows, :] = jnp.where(low, q, zero)
        qm[1, rows, :] = jnp.where(low, zero, q)
        dom[0, rows, :] = jnp.where(low, do, zero)
        dom[1, rows, :] = jnp.where(low, zero, do)
        kt[:, rows] = k_ref[rows, :].astype(F32).T.astype(BF16)
        prod = do.astype(F32).T * ctxt_ref[:, rows]
        delta[0:1, rows] = jnp.sum(prod[0:HEAD_DIM, :], axis=0, keepdims=True)
        delta[1:2, rows] = jnp.sum(prod[HEAD_DIM:, :], axis=0, keepdims=True)
        dqt[:, rows] = jnp.zeros((width, tile), F32)

    diag = lax.broadcasted_iota(jnp.int32, (tile, tile), 0) <= lax.broadcasted_iota(
        jnp.int32, (tile, tile), 1
    )

    @pl.loop(0, n_tiles)
    def _(j):
        sc.later(j + 1, sum_ref)
        rows_k = pl.ds(pl.multiple_of(j * tile, tile), tile)
        keys = k_ref[rows_k, :]
        vals = v_ref[rows_k, :]

        def step(i, carry, masked):
            rows_q = pl.ds(pl.multiple_of(i * tile, tile), tile)
            dk, dv = carry
            for h in range(2):
                s = dot_nt(keys, qm[h, rows_q, :]) * EXP2_SCALE
                p = jnp.exp2(s - lse_ref[h : h + 1, rows_q])
                if masked:
                    p = jnp.where(diag, p, 0.0)
                dp = dot_nt(vals, dom[h, rows_q, :])
                ds = (p * (dp - delta[h : h + 1, rows_q])).astype(BF16)
                dv = dv + dot_nn(p.astype(BF16), dom[h, rows_q, :])
                dk = dk + dot_nn(ds, qm[h, rows_q, :])
                part = slice(h * HEAD_DIM, (h + 1) * HEAD_DIM)
                dqt[part, rows_q] += dot_nn(kt[part, rows_k], ds)
            return dk, dv

        zero = jnp.zeros((tile, width), F32)
        carry = step(j, (zero, zero), True)
        dk, dv = lax.fori_loop(j + 1, n_tiles, lambda i, c: step(i, c, False), carry)
        dk_buf[rows_k, :] = (dk * scale).astype(BF16)
        dv_buf[rows_k, :] = dv.astype(BF16)

    @pl.loop(0, n_tiles)
    def _(t):
        rows = pl.ds(pl.multiple_of(t * tile, tile), tile)
        do_sorted[rows, :] = (dqt[:, rows].T * scale).astype(BF16)

    @pl.loop(0, n_blocks)
    def _(b):
        src = pl.ds(pl.multiple_of(b * block, block), block)
        cos, sin = rope_of_block(base_ref, step_ref, b)
        dq = do_sorted[src, :].astype(F32)
        dk = dk_buf[src, :].astype(F32)
        d_blocks[b, :, 0:width] = (dq * cos - swap_halves(dq) * sin).astype(BF16)
        d_blocks[b, :, width : 2 * width] = (dk * cos - swap_halves(dk) * sin).astype(BF16)
        d_blocks[b, :, 2 * width : 3 * width] = dv_buf[src, :]

    @pl.loop(0, n_blocks)
    def _(t):
        out_ref[t] = d_blocks[order_ref[t]]

    def x_load(p):
        return pltpu.make_async_copy(xn_ref.at[p], x_buf.at[p % 2], l_x.at[p % 2])

    pairs = xn_ref.shape[0]
    x_load(0).start()
    acc[...] = jnp.zeros_like(acc)

    @pl.loop(n_tiles + 1, sc.steps)
    def _(k):
        for j in range(2):
            p = 2 * (k - n_tiles - 1) + j

            @pl.when(p < pairs)
            def _():
                @pl.when(p + 1 < pairs)
                def _():
                    x_load(p + 1).start()

                x_load(p).wait()
                d_pair = out_ref[pl.ds(2 * p, 2)].reshape(2 * block, 3 * width)
                acc[...] += dot_tn(x_buf[p % 2], d_pair)

        sc.later(k, sum_ref)

    gq_ref[...] = acc[...].astype(BF16)
    moves.drain()
    sc.drain()

    @pl.loop(1, n_dp)
    def _(r):
        x_copy(r).wait()


def attn_bwd(
    slot_of_block, order, q, k, v, d_ctx, ctxt, lse, base, step, partial, grad_out, xn, nz, tile
):
    length, width = q.shape
    block, wide = d_ctx.shape
    whole = pl.BlockSpec(memory_space=pltpu.VMEM)
    smem = pl.BlockSpec(memory_space=pltpu.SMEM)
    any_spec = pl.BlockSpec(memory_space=pl.ANY)
    n_dp = grad_out.shape[0]
    d_qkv, summed, grad_out_in, grad_qkv = pl.pallas_call(
        functools.partial(attn_bwd_kernel, nz, n_dp, block, tile),
        in_specs=[smem, smem] + [whole] * 3 + [any_spec] + [whole] * 4 + [any_spec] * 3,
        out_specs=[whole, whole, any_spec, whole],
        out_shape=[
            jax.ShapeDtypeStruct((length // block, block, 3 * width), BF16),
            jax.ShapeDtypeStruct((block, wide), F32),
            jax.ShapeDtypeStruct(grad_out.shape, BF16),
            jax.ShapeDtypeStruct((wide, 3 * width), BF16),
        ],
        scratch_shapes=[
            pltpu.VMEM((2, length, width), BF16),
            pltpu.VMEM((2, length, width), BF16),
            pltpu.VMEM((length // block, block, width), BF16),
            pltpu.VMEM((length, width), BF16),
            pltpu.VMEM((width, length), BF16),
            pltpu.VMEM((2, length), F32),
            pltpu.VMEM((width, length), F32),
            pltpu.VMEM((length, width), BF16),
            pltpu.VMEM((length, width), BF16),
            pltpu.VMEM((length // block, block, 3 * width), BF16),
            pltpu.VMEM((wide, 3 * width), F32),
            pltpu.VMEM((2, 2 * block, wide), BF16),
            pltpu.SemaphoreType.DMA((2,)),
            pltpu.SemaphoreType.DMA((nz * CHUNKS,)),
            pltpu.SemaphoreType.DMA((n_dp,)),
            pltpu.SemaphoreType.DMA((n_dp,)),
        ]
        + scatter_buffers(nz, block, wide)
        + exchange_sems(nz)
        + scatter_sems(nz),
        compiler_params=pltpu.CompilerParams(
            vmem_limit_bytes=VMEM_LIMIT, collective_id=6, has_side_effects=True
        ),
        cost_estimate=pl.CostEstimate(
            flops=50 * length * length * HEAD_DIM,
            bytes_accessed=60 * length * wide,
            transcendentals=length * length,
        ),
        name="attn_bwd",
    )(
        slot_of_block, order, q, k, v, d_ctx, ctxt, lse, base, step,
        partial.reshape(nz, 2, 2, block, wide), grad_out, xn.reshape(2 * nz, 2 * block, wide),
    )
    return d_qkv.reshape(length, 3 * width), summed, grad_out_in, grad_qkv


def scatter_mlp_kernel(
    nz, p_ref, x_ref, c_ref, dgu_ref, hid_ref,
    out_ref, grad_ref,
    acc, x_buf, c_buf, dgu_buf, hid_buf, l_m, l_x, l_c, l_g, l_h, *rest,
):
    bufs, sems = rest[:4], rest[4:]
    mine = bufs[0]
    pairs = x_ref.shape[0]
    gate_up = dgu_ref.shape[2]
    tile = 512 if acc.shape[0] % 512 == 0 else acc.shape[0]

    sc = Scatter(lambda zs, part: p_ref.at[zs, :, 1 - sc.c, part, :], bufs, sems, nz)

    def load(k):
        zs, part = sc.unit(k)
        return pltpu.make_async_copy(
            p_ref.at[zs, :, sc.c, part, :], mine.at[zs, :, part, :], l_m.at[k]
        )

    def operands(k):
        s = k % 2
        return [
            pltpu.make_async_copy(ref.at[k], buf.at[s], sem.at[s])
            for ref, buf, sem in (
                (x_ref, x_buf, l_x),
                (c_ref, c_buf, l_c),
                (dgu_ref, dgu_buf, l_g),
                (hid_ref, hid_buf, l_h),
            )
        ]

    greet_neighbours(nz)

    @pl.loop(0, sc.units)
    def _(k):
        sc.to_sibling(k).start()
        load(k).start()

    for copy in operands(0):
        copy.start()
    acc[...] = jnp.zeros_like(acc)

    def weight_grads(k):
        @pl.when(k + 1 < pairs)
        def _():
            for copy in operands(k + 1):
                copy.start()

        for copy in operands(k):
            copy.wait()
        s = k % 2

        @pl.loop(0, acc.shape[0] // tile)
        def _(t):
            at = pl.ds(pl.multiple_of(t * tile, tile), tile)
            acc[at, 0:gate_up] += dot_tn(x_buf[s, :, at], dgu_buf[s])
            acc[at, gate_up:] += dot_tn(c_buf[s, :, at], hid_buf[s])

    @pl.loop(0, sc.steps)
    def _(k):
        @pl.when(k < sc.units)
        def _():
            load(k).wait()

        sc.step(k, out_ref)

        @pl.when(k < pairs)
        def _():
            weight_grads(k)

    grad_ref[...] = acc[...].astype(BF16)
    sc.drain()


def scatter_mlp(partial, x_all, c_all, d_gu, hid, nz, collective_id):
    rows, width = partial.shape[0] // (nz * 4), partial.shape[1]
    hidden = hid.shape[1]
    pairs = 2 * nz
    any_spec = pl.BlockSpec(memory_space=pl.ANY)
    vmem = pl.BlockSpec(memory_space=pltpu.VMEM)
    dma = pltpu.SemaphoreType.DMA

    def by_pair(a):
        return a.reshape(pairs, 2 * rows, a.shape[1])

    def buffers(cols):
        return pltpu.VMEM((2, 2 * rows, cols), BF16)

    return pl.pallas_call(
        functools.partial(scatter_mlp_kernel, nz),
        in_specs=[any_spec] * 5,
        out_specs=[vmem, vmem],
        out_shape=[
            jax.ShapeDtypeStruct((rows, width), F32),
            jax.ShapeDtypeStruct((width, 3 * hidden), BF16),
        ],
        scratch_shapes=[
            pltpu.VMEM((width, 3 * hidden), F32),
            buffers(width),
            buffers(width),
            buffers(2 * hidden),
            buffers(hidden),
            dma((nz * CHUNKS,)),
            dma((2,)),
            dma((2,)),
            dma((2,)),
            dma((2,)),
        ]
        + scatter_buffers(nz, rows, width)
        + scatter_sems(nz),
        compiler_params=pltpu.CompilerParams(
            vmem_limit_bytes=VMEM_LIMIT, collective_id=collective_id, has_side_effects=True
        ),
        cost_estimate=pl.CostEstimate(
            flops=6 * partial.size * hidden,
            bytes_accessed=60 * partial.size,
            transcendentals=0,
        ),
        name="scatter_mlp",
    )(
        partial.reshape(nz, 2, 2, rows, width),
        by_pair(x_all),
        by_pair(c_all),
        by_pair(d_gu),
        by_pair(hid),
    )


def scatter_last_kernel(
    nz, n_dp, dq_ref, w_ref, gq_ref, gm_ref, go_ref, go_in,
    out_ref, gq_out, gm_out,
    theirs, gq_in, gq_sum, gm_in, gm_sum, go_buf,
    l_o, l_q, s_xq, r_xq, own_q, s_q, r_q, l_m, s_xm, r_xm, own_m, s_m, r_m, *rest,
):
    bufs, sems = rest[:4], rest[4:]
    sc = Scatter(lambda zs, part: theirs.at[zs, :, part, :], bufs, sems, nz)
    mine = bufs[0]
    d = lax.axis_index("dp")
    rows, width = dq_ref.shape[3], mine.shape[3]
    shard = gq_in.shape[2]
    cols = dq_ref.shape[4]
    gq_moves = Exchange(
        lambda t: gq_sum.at[t], lambda t: gq_out.at[t], (s_q, r_q, own_q), nz
    )
    gm_moves = Exchange(
        lambda t: gm_sum.at[t], lambda t: gm_out.at[t], (s_m, r_m, own_m), nz
    )

    keep_q = pltpu.make_async_copy(gq_ref.at[d], gq_in.at[0], l_q)
    keep_q.start()
    keep_m = pltpu.make_async_copy(gm_ref.at[d], gm_sum, l_m)
    keep_m.start()

    def xq_copy(r):
        t = (d + r) % n_dp
        return remote(gq_ref.at[t], gq_in.at[r], s_xq.at[r], r_xq.at[r], dp=t)

    def xm_copy(i, r):
        t = (gm_moves.me + i) % gm_moves.peers
        dp = (d + r) % n_dp
        return remote(gm_ref.at[dp, t], gm_in.at[r - 1, t], s_xm.at[i, r], r_xm.at[i, r], dp=dp)

    greet_all(nz, n_dp)

    @pl.loop(1, n_dp)
    def _(r):
        xq_copy(r).start()

        @pl.loop(1, gm_moves.peers + 1)
        def _(i):
            xm_copy(i, r).start()

    def partial_sums(zs, core):
        left = dq_ref[zs, :, core].reshape(2 * rows, cols)
        return dot_nt(left, w_ref[:, 0:cols]).astype(BF16).reshape(2, rows, width)

    def out_loads(zs):
        own = pltpu.make_async_copy(go_ref.at[d, zs], go_buf.at[0], l_o.at[0])
        return [own] + [
            pltpu.make_async_copy(go_in.at[r, zs], go_buf.at[r], l_o.at[r]) for r in range(1, n_dp)
        ]

    def out_sums(core):
        return sum(go_buf[r, :, core].astype(F32) for r in range(n_dp)).astype(BF16)

    if mine.shape[2] > rows + shard:
        for buf in (mine, theirs):
            buf[:, :, rows + shard :, :] = jnp.zeros_like(buf[:, :, rows + shard :, :])

    def produce(i):
        zs = jnp.where(i % 2 == 0, nz - 1 - i // 2, i // 2)
        for copy in out_loads(zs):
            copy.start()
        theirs[zs, :, 0:rows, :] = partial_sums(zs, 1 - sc.c)
        for copy in out_loads(zs):
            copy.wait()
        theirs[zs, :, rows : rows + shard, :] = out_sums(1 - sc.c)
        for q in range(CHUNKS):
            sc.to_sibling(2 * CHUNKS * (i // 2) + 2 * q + i % 2).start()
        mine[zs, :, 0:rows, :] = partial_sums(zs, sc.c)
        mine[zs, :, rows : rows + shard, :] = out_sums(sc.c)

    @pl.loop(0, 2)
    def _(i):
        produce(i)

    keep_m.wait()

    def mlp_block(i):
        t = (gm_moves.me + i) % gm_moves.peers
        @pl.loop(1, n_dp)
        def _(r):
            xm_copy(i, r).wait_recv()
            gm_sum[t] = (gm_sum[t].astype(F32) + gm_in[r - 1, t].astype(F32)).astype(BF16)

        @pl.when(i < gm_moves.peers)
        def _():
            gm_moves.copy(i).start()

        @pl.when(i == gm_moves.peers)
        def _():
            gm_moves.keep().start()

    @pl.loop(0, sc.steps)
    def _(k):
        sc.step(k, out_ref)

        @pl.when(k < nz - 2)
        def _():
            produce(k + 2)

        @pl.when(k == 1)
        def _():
            keep_q.wait()
            gq_sum[...] = gq_in[0]

            @pl.loop(1, n_dp)
            def _(r):
                xq_copy(r).wait_recv()
                gq_sum[...] = (gq_sum[...].astype(F32) + gq_in[r].astype(F32)).astype(BF16)

            gq_moves.start()

        for j in range(2):
            i = 2 * (k - 2) + 1 + j

            @pl.when(jnp.logical_and(i >= 1, i <= gm_moves.peers))
            def _():
                mlp_block(i)

    sc.drain()
    for moves in (gq_moves, gm_moves):
        moves.arrive()
        moves.drain()

    @pl.loop(1, n_dp)
    def _(r):
        xq_copy(r).wait_send()

        @pl.loop(1, gm_moves.peers + 1)
        def _(i):
            xm_copy(i, r).wait_send()


def scatter_last(d_qkv, w, grad_qkv, grad_mlp, grad_out, grad_out_in, nz, n_dp, collective_id):
    peers = nz * 4
    rows, cols = d_qkv.shape[0] // peers, d_qkv.shape[1]
    width = w.shape[0]
    shard = width // (n_dp * peers)
    cols_mlp = grad_mlp.shape[1]
    all_rows = rows + max(shard, 16 * CHUNKS)
    any_spec = pl.BlockSpec(memory_space=pl.ANY)
    vmem = pl.BlockSpec(memory_space=pltpu.VMEM)
    dma = pltpu.SemaphoreType.DMA
    return pl.pallas_call(
        functools.partial(scatter_last_kernel, nz, n_dp),
        in_specs=[vmem, vmem] + [any_spec] * 4,
        out_specs=[vmem, any_spec, any_spec],
        out_shape=[
            jax.ShapeDtypeStruct((all_rows, width), F32),
            jax.ShapeDtypeStruct((peers, shard, cols), BF16),
            jax.ShapeDtypeStruct((peers, shard, cols_mlp), BF16),
        ],
        scratch_shapes=[
            pltpu.VMEM((nz, 2, all_rows, width), BF16),
            pltpu.VMEM((n_dp, peers, shard, cols), BF16),
            pltpu.VMEM((peers, shard, cols), BF16),
            pltpu.VMEM((n_dp - 1, peers, shard, cols_mlp), BF16),
            pltpu.VMEM((peers, shard, cols_mlp), BF16),
            pltpu.VMEM((n_dp, 2, 2, shard, width), BF16),
            dma((n_dp,)),
            dma,
            dma((n_dp,)),
            dma((n_dp,)),
            dma,
            dma((peers,)),
            dma((peers,)),
            dma,
            dma((peers + 1, n_dp)),
            dma((peers + 1, n_dp)),
            dma,
            dma((peers,)),
            dma((peers,)),
        ]
        + scatter_buffers(nz, all_rows, width)
        + scatter_sems(nz),
        compiler_params=pltpu.CompilerParams(
            vmem_limit_bytes=VMEM_LIMIT, collective_id=collective_id, has_side_effects=True
        ),
        cost_estimate=pl.CostEstimate(
            flops=2 * peers * rows * width * cols,
            bytes_accessed=60 * peers * rows * width,
            transcendentals=0,
        ),
        name="scatter_last",
    )(
        d_qkv.reshape(nz, 2, 2, rows, cols),
        w,
        grad_qkv.reshape(n_dp, peers, shard, cols),
        grad_mlp.reshape(n_dp, peers, shard, cols_mlp),
        grad_out.reshape(n_dp, nz, 2, 2, shard, width),
        grad_out_in.reshape(n_dp, nz, 2, 2, shard, width),
    )


def layout_kernel(
    gq_ref, gm_ref, wq_ref, wgu_ref, g1_ref, g2_ref, q_out, gu_out, down_out, g1_out, g2_out
):
    peers = gq_ref.shape[0]
    part_q = gq_ref.shape[2] // 3
    hid = gm_ref.shape[2] // 3
    sum_q = jnp.zeros((gq_ref.shape[1], part_q), F32)
    sum_m = jnp.zeros((gq_ref.shape[1], hid), F32)
    for t in range(peers):
        for s in range(3):
            at = pl.ds((s * peers + t) * part_q, part_q)
            block = gq_ref[t, :, s * part_q : (s + 1) * part_q].astype(F32)
            q_out[:, at] = block
            sum_q += block * wq_ref[:, at].astype(F32)
        for s in range(2):
            at = pl.ds((s * peers + t) * hid, hid)
            block = gm_ref[t, :, s * hid : (s + 1) * hid].astype(F32)
            gu_out[:, at] = block
            sum_m += block * wgu_ref[:, at].astype(F32)
        down_out[:, t * hid : (t + 1) * hid] = gm_ref[t, :, 2 * hid :].astype(F32)
    g1_out[...] = jnp.sum(sum_q, axis=1, keepdims=True) / g1_ref[...].astype(F32)
    g2_out[...] = jnp.sum(sum_m, axis=1, keepdims=True) / g2_ref[...].astype(F32)


def layout_call(grad_qkv, grad_mlp, w_qkv, w_gate_up, gain_one, gain_two):
    shard = w_qkv.shape[0]
    hidden = w_gate_up.shape[1] // 2
    vmem = pl.BlockSpec(memory_space=pltpu.VMEM)
    return pl.pallas_call(
        layout_kernel,
        in_specs=[vmem] * 6,
        out_specs=[vmem] * 5,
        out_shape=[
            jax.ShapeDtypeStruct(w_qkv.shape, F32),
            jax.ShapeDtypeStruct(w_gate_up.shape, F32),
            jax.ShapeDtypeStruct((shard, hidden), F32),
            jax.ShapeDtypeStruct((shard, 1), F32),
            jax.ShapeDtypeStruct((shard, 1), F32),
        ],
        compiler_params=pltpu.CompilerParams(vmem_limit_bytes=VMEM_LIMIT),
        name="layout",
    )(grad_qkv, grad_mlp, w_qkv, w_gate_up, gain_one[:, None], gain_two[:, None])


def gather_qkv_kernel(
    nz, n_dp, tok_ref, wq_ref, wgu_ref, wd_ref, wo_ref,
    xn_ref, qkv_ref, gain_ref, wq_out, wm_out, wo_out,
    g, wq, xn_stage, own_sem, s_w, r_w, s_d, r_d, s_m, r_m, own_w, own_m, own_o, o_xn, o_w,
    *sems,
):
    peers = nz * 4
    gather = Gather(g, sems[:7], nz)
    w_out = DpGather(wo_out, sems[7:], nz, n_dp)
    z, y, c = gather.z, gather.y, gather.c
    me = z * 4 + y * 2 + c
    d = lax.axis_index("dp")
    pair_rows = 2 * tok_ref.shape[0]
    cols = qkv_ref.shape[2]
    shard = wq_ref.shape[1]
    hid = wd_ref.shape[1] // peers

    def block_rows(dp, t):
        return pl.ds(pl.multiple_of((dp * peers + t) * shard, shard), shard)

    def plane_rows(dp):
        return pl.ds(pl.multiple_of(dp * (peers * shard), peers * shard), peers * shard)

    def mlp_part(t, s):
        first = t * hid if s != 1 else (peers + t) * hid
        cols_t = pl.ds(pl.multiple_of(first, hid), hid)
        return (wd_ref if s == 2 else wgu_ref).at[:, cols_t]

    def mlp_place(t, s):
        return wm_out.at[block_rows(0, t), pl.ds(s * hid, hid)]

    own = pltpu.make_async_copy(tok_ref, g.at[z, y, c], own_sem)
    own.start()
    keep_w = pltpu.make_async_copy(wq_ref.at[me], wq.at[block_rows(d, me), :], own_w)
    keep_w.start()
    keep_o = pltpu.make_async_copy(wo_ref, wo_out.at[d, z, y, c], own_o)
    keep_o.start()
    keep_m = [
        pltpu.make_async_copy(mlp_part(me, s), mlp_place(me, s), own_m.at[s]) for s in range(3)
    ]
    for copy in keep_m:
        copy.start()

    greet_all(nz, n_dp)

    def place(t):
        return {"hs": t // 4, "blk": t % 4}

    def w_copy(r):
        t = (me + r) % peers
        return remote(
            wq_ref.at[t], wq.at[block_rows(d, me), :], s_w.at[r], r_w.at[r], **place(t)
        )

    def w_take(r):
        t = (me + peers - r) % peers
        p = wq.at[block_rows(d, t), :]
        return remote(p, p, s_w.at[r], r_w.at[r], **place(t))

    def m_copy(r, s):
        t = (me + r) % peers
        return remote(
            mlp_part(t, s), mlp_place(me, s), s_m.at[r, s], r_m.at[r, s], **place(t)
        )

    def m_take(r, s):
        t = (me + peers - r) % peers
        p = mlp_place(t, s)
        return remote(p, p, s_m.at[r, s], r_m.at[r, s], **place(t))

    def d_copy(r):
        p = wq.at[plane_rows(d), :]
        return remote(p, p, s_d.at[r], r_d.at[r], dp=(d + r) % n_dp)

    def d_take(r):
        p = wq.at[plane_rows((d + n_dp - r) % n_dp), :]
        return remote(p, p, s_d.at[r], r_d.at[r], dp=(d + r) % n_dp)

    def mlp_sends(first, last):
        @pl.loop(first, last)
        def _(r):
            for s in range(3):
                m_copy(r, s).start()

    own.wait()
    gather.row_step(0)

    @pl.loop(1, peers)
    def _(r):
        w_copy(r).start()

    keep_o.wait()
    w_out.row_step(0)
    third = peers // 3
    mlp_sends(1, 1 + third)
    gather.row_step(1)
    gather.cross_step(0)
    mlp_sends(1 + third, 1 + 2 * third)
    w_out.row_step(1)
    w_out.cross_step(0)

    @pl.loop(1, peers)
    def _(r):
        w_take(r).wait_recv()

    keep_w.wait()

    @pl.loop(1, n_dp)
    def _(r):
        d_copy(r).start()

    @pl.loop(2, nz)
    def _(n):
        gather.row_step(n)
        gather.cross_step(n - 1)

        @pl.when(n == 2)
        def _():
            mlp_sends(1 + 2 * third, peers)

        w_out.row_step(n)
        w_out.cross_step(n - 1)

    @pl.loop(1, n_dp)
    def _(r):
        d_take(r).wait_recv()

    gain_ref[...] = wq[:, cols:].astype(F32).T[0:8, :]
    keep_out = pltpu.make_async_copy(wq, wq_out, o_w)
    keep_out.start()
    gain = gain_ref[0:1, :]

    def xn_copy(m, pair):
        return pltpu.make_async_copy(xn_stage.at[m % 2], xn_ref.at[pair], o_xn.at[m % 2])

    @pl.loop(0, 2 * nz)
    def _(m):
        zs = by_distance(z, m // 2, nz)
        yy = jnp.where(m % 2 == 0, y, 1 - y)
        pair = zs * 2 + yy

        @pl.when(m == 2 * nz - 1)
        def _():
            gather.cross_step(nz - 1)
            w_out.cross_step(nz - 1)

        gather.ready(zs, yy)

        @pl.when(m >= 2)
        def _():
            xn_copy(m, pair).wait()

        x = g[zs, yy].reshape(pair_rows, g.shape[4]).astype(F32)
        xn = rms_scale(x, gain).astype(BF16)
        xn_stage[m % 2] = xn
        xn_copy(m, pair).start()
        qkv_ref[pair] = dot_nn(xn, wq[:, 0:cols])

    w_out.finish()
    for m in range(2):
        xn_copy(m, 0).wait()
    gather.drain()
    keep_out.wait()

    @pl.loop(1, peers)
    def _(r):
        w_copy(r).wait_send()
        for s in range(3):
            m_copy(r, s).wait_send()
            m_take(r, s).wait_recv()

    for copy in keep_m:
        copy.wait()

    @pl.loop(1, n_dp)
    def _(r):
        d_copy(r).wait_send()


def gather_qkv(tokens, wq_parts, w_gate_up, w_down, w_out, nz, n_dp, cols):
    rows, width = tokens.shape
    peers, shard, wide = wq_parts.shape
    hid = w_down.shape[1] // peers
    any_spec = pl.BlockSpec(memory_space=pl.ANY)
    vmem = pl.BlockSpec(memory_space=pltpu.VMEM)
    dma = pltpu.SemaphoreType.DMA
    length = peers * rows
    xn, qkv, gains, wq, wm, wo = pl.pallas_call(
        functools.partial(gather_qkv_kernel, nz, n_dp),
        in_specs=[any_spec] * 5,
        out_specs=[any_spec, vmem, vmem, any_spec, any_spec, any_spec],
        out_shape=[
            jax.ShapeDtypeStruct((peers // 2, 2 * rows, width), BF16),
            jax.ShapeDtypeStruct((peers // 2, 2 * rows, cols), F32),
            jax.ShapeDtypeStruct((8, width), F32),
            jax.ShapeDtypeStruct((width, wide), BF16),
            jax.ShapeDtypeStruct((width // n_dp, 3 * hid), BF16),
            jax.ShapeDtypeStruct((n_dp, nz, 2, 2, shard, width), BF16),
        ],
        scratch_shapes=[
            pltpu.VMEM((nz, 2, 2, rows, width), BF16),
            pltpu.VMEM((n_dp * peers * shard, wide), BF16),
            pltpu.VMEM((2, 2 * rows, width), BF16),
            dma,
            dma((peers,)),
            dma((peers,)),
            dma((n_dp,)),
            dma((n_dp,)),
            dma((peers, 3)),
            dma((peers, 3)),
            dma,
            dma((3,)),
            dma,
            dma((2,)),
            dma,
        ]
        + gather_sems(nz)
        + dp_gather_sems(nz, n_dp),
        compiler_params=pltpu.CompilerParams(
            vmem_limit_bytes=VMEM_LIMIT, collective_id=1, has_side_effects=True
        ),
        cost_estimate=pl.CostEstimate(
            flops=2 * length * width * cols,
            bytes_accessed=60 * length * width,
            transcendentals=0,
        ),
        name="gather_qkv",
    )(tokens, wq_parts, w_gate_up, w_down, w_out)
    return (
        xn.reshape(length, width), qkv.reshape(length, cols), gains, wq, wm,
        wo.reshape(width, width),
    )


def gather_mlp_kernel(
    nz, n_dp, x_ref, c_ref, wm_ref, wm_in,
    xn_ref, out_ref, dx_ref, hid_ref, dgu_ref,
    g, w_ref, c_buf, out_buf, dx_buf, hid_buf, dgu_buf,
    w_sem, own_sem, c_sem, x_sem, out_sem, dx_sem, hid_sem, dgu_sem, *sems,
):
    gather = Gather(g, sems, nz)
    z, y, c = gather.z, gather.y, gather.c
    hidden = w_ref.shape[1] // 3
    w_gate, w_up, w_down = (pl.ds(i * hidden, hidden) for i in range(3))
    pair_rows = 2 * x_ref.shape[0]
    steps = 2 * nz

    own = pltpu.make_async_copy(x_ref, g.at[z, y, c], own_sem)
    own.start()
    d = lax.axis_index("dp")
    half = wm_ref.shape[0]

    def w_load(r):
        start = pl.multiple_of(((d + n_dp - r) % n_dp) * half, half)
        src = wm_ref if r == 0 else wm_in.at[r - 1]
        return pltpu.make_async_copy(src, w_ref.at[pl.ds(start, half), :], w_sem.at[r])

    for r in range(n_dp):
        w_load(r).start()

    def place(m):
        return by_distance(z, m // 2, nz), jnp.where(m % 2 == 0, y, 1 - y)

    def pair(m):
        zs, yy = place(m)
        return zs * 2 + yy

    def c_copy(m):
        return pltpu.make_async_copy(c_ref.at[pair(m)], c_buf.at[m % 2], c_sem.at[m % 2])

    def x_copy(m):
        zs, yy = place(m)
        return pltpu.make_async_copy(g.at[zs, yy], xn_ref.at[zs, yy], x_sem.at[m])

    def results(m):
        s = m % 2
        return [
            pltpu.make_async_copy(buf.at[s], ref.at[pair(m)], sem.at[s])
            for buf, ref, sem in (
                (out_buf, out_ref, out_sem),
                (dx_buf, dx_ref, dx_sem),
                (hid_buf, hid_ref, hid_sem),
                (dgu_buf, dgu_ref, dgu_sem),
            )
        ]

    c_copy(0).start()
    greet_neighbours(nz)
    own.wait()
    gather.row_step(0)
    for r in range(n_dp):
        w_load(r).wait()

    @pl.loop(0, steps)
    def _(m):
        @pl.when(m % 2 == 1)
        def _():
            n = (m + 1) // 2

            @pl.when(n < nz)
            def _():
                gather.row_step(n)

            gather.cross_step(n - 1)

        zs, yy = place(m)
        gather.ready(zs, yy)
        x_copy(m).start()

        @pl.when(m + 1 < steps)
        def _():
            c_copy(m + 1).start()

        @pl.when(m >= 2)
        def _():
            for copy in results(m - 2):
                copy.wait()

        c_copy(m).wait()
        s = m % 2
        x = g[zs, yy].reshape(pair_rows, g.shape[4])
        gate = dot_nn(x, w_ref[:, w_gate])
        up = dot_nn(x, w_ref[:, w_up])
        d_hid = dot_nn(c_buf[s], w_ref[:, w_down])
        sigma = 1.0 / (1.0 + jnp.exp(-gate))
        act = gate * sigma
        hid = (act * up).astype(BF16)
        d_gate = (d_hid * up * (sigma * (1.0 + gate * (1.0 - sigma)))).astype(BF16)
        d_up = (d_hid * act).astype(BF16)
        hid_buf[s] = hid
        dgu_buf[s, :, 0:hidden] = d_gate
        dgu_buf[s, :, hidden:] = d_up
        dx = dot_nt(d_gate, w_ref[:, w_gate]) + dot_nt(d_up, w_ref[:, w_up])
        dx_buf[s] = dx.astype(BF16)
        out_buf[s] = dot_nt(hid, w_ref[:, w_down]).astype(BF16)
        for copy in results(m):
            copy.start()

    for m in (steps - 2, steps - 1):
        for copy in results(m):
            copy.wait()

    @pl.loop(0, steps)
    def _(m):
        x_copy(m).wait()

    gather.drain()


def gather_mlp(xn, c_all, wm, wm_in, nz, n_dp):
    rows, width = xn.shape
    hidden = wm.shape[1] // 3
    pairs = nz * 2
    length = 2 * pairs * rows
    any_spec = pl.BlockSpec(memory_space=pl.ANY)
    dma = pltpu.SemaphoreType.DMA

    def by_pair(cols):
        return jax.ShapeDtypeStruct((pairs, 2 * rows, cols), BF16)

    def buffers(cols):
        return pltpu.VMEM((2, 2 * rows, cols), BF16)

    xn_all, out_part, dx_part, hid, d_gu = pl.pallas_call(
        functools.partial(gather_mlp_kernel, nz, n_dp),
        in_specs=[any_spec] * 4,
        out_specs=[any_spec] * 5,
        out_shape=[
            jax.ShapeDtypeStruct((nz, 2, 2, rows, width), BF16),
            by_pair(width),
            by_pair(width),
            by_pair(hidden),
            by_pair(2 * hidden),
        ],
        scratch_shapes=[
            pltpu.VMEM((nz, 2, 2, rows, width), BF16),
            pltpu.VMEM((width, 3 * hidden), BF16),
            buffers(width),
            buffers(width),
            buffers(width),
            buffers(hidden),
            buffers(2 * hidden),
            dma((n_dp,)),
            dma,
            dma((2,)),
            dma((pairs,)),
            dma((2,)),
            dma((2,)),
            dma((2,)),
            dma((2,)),
        ]
        + gather_sems(nz),
        compiler_params=pltpu.CompilerParams(
            vmem_limit_bytes=VMEM_LIMIT, collective_id=2, has_side_effects=True
        ),
        cost_estimate=pl.CostEstimate(
            flops=12 * length * width * hidden,
            bytes_accessed=60 * length * width,
            transcendentals=length * hidden,
        ),
        name="gather_mlp",
    )(xn, c_all.reshape(pairs, 2 * rows, width), wm, wm_in)
    return (
        xn_all.reshape(length, width),
        out_part.reshape(length, width),
        dx_part.reshape(length, width),
        hid.reshape(length, hidden),
        d_gu.reshape(length, 2 * hidden),
    )


def by_group(weight, groups, sections):
    rows, cols = weight.shape
    part = cols // (groups * sections)
    parts = weight.reshape(rows, sections, groups, part)
    return jnp.transpose(parts, (2, 0, 1, 3)).reshape(groups, rows, sections * part)


def body(tokens, block_order, gain_attn, w_qkv, w_out, gain_mlp, w_gate_up, w_down, cotangent):
    nz = lax.axis_size("hs")
    groups = nz * lax.axis_size("blk")
    n_dp = lax.axis_size("dp")
    tok_rows, width = tokens.shape
    shard = w_qkv.shape[0]
    length = groups * tok_rows

    order = block_order[0]
    slot_of_block = jnp.argsort(order).astype(jnp.int32)
    base, step = rope_tables(groups, tok_rows)

    gain_columns = jnp.pad(jnp.stack([gain_attn, gain_mlp], axis=1), ((0, 0), (0, 126)))
    wq_parts = jnp.concatenate(
        [
            by_group(w_qkv, groups, 3),
            jnp.broadcast_to(gain_columns[None], (groups,) + gain_columns.shape),
        ],
        axis=2,
    )
    xn1_all, qkv, gains, wqkv_mine, wmlp_mine, wout_full = gather_qkv(
        tokens, wq_parts, w_gate_up, w_down, w_out, nz, n_dp, 3 * width // groups
    )

    q, k, v, ctxt, lse, ctx_tok, cot_all, wmlp_other = attn_fwd(
        slot_of_block, order, qkv, base, step, cotangent, wmlp_mine, nz, n_dp, 512
    )

    x_float = tokens.astype(F32)
    gain_one, gain_two = gains[0], gains[1]
    y_mid = x_float + dot_nn(ctx_tok, wout_full)
    xn2 = rms_scale(y_mid, gain_two).astype(BF16)

    xn2_all, out_part, dx_part, hid, d_gu = gather_mlp(
        xn2, cot_all, wmlp_mine, wmlp_other, nz, n_dp
    )
    d_xn2, grad_mlp = scatter_mlp(dx_part, xn2_all, cot_all, d_gu, hid, nz, 3)
    _, pull_two = jax.vjp(lambda v: rms_scale(v, gain_two), y_mid)
    (dy_norm,) = pull_two(d_xn2)
    d_mid = cotangent.astype(F32) + dy_norm
    d_mid_b = d_mid.astype(BF16)

    d_ctx = dot_nt(d_mid_b, wout_full).astype(BF16)
    grad_out = dot_tn(ctx_tok, d_mid_b).astype(BF16).reshape(n_dp, groups * shard, width)

    d_qkv, mlp_out, grad_out_in, grad_qkv = attn_bwd(
        slot_of_block, order, q, k, v, d_ctx, ctxt, lse, base, step, out_part, grad_out, xn1_all,
        nz, 512,
    )
    layer_out = (y_mid + mlp_out).astype(BF16)
    sums, grad_qkv, grad_mlp = scatter_last(
        d_qkv, wqkv_mine, grad_qkv, grad_mlp, grad_out, grad_out_in, nz, n_dp, 4
    )
    d_xn1, out_rows = sums[:tok_rows], sums[tok_rows : tok_rows + shard]
    qkv_rows, gu_rows, down_rows, grad_gain_one, grad_gain_two = layout_call(
        grad_qkv, grad_mlp, w_qkv, w_gate_up, gain_attn, gain_mlp
    )

    _, pull_one = jax.vjp(lambda v: rms_scale(v, gain_one), x_float)
    (dx_norm,) = pull_one(d_xn1)
    grad_tokens = d_mid + dx_norm
    return (
        layer_out,
        grad_tokens,
        grad_gain_one.reshape(shard),
        qkv_rows,
        out_rows,
        grad_gain_two.reshape(shard),
        gu_rows,
        down_rows,
    )


def solution(mesh):
    rows = P(ALL, None)
    in_specs = (rows, P("dp", None), P(ALL), rows, rows, P(ALL), rows, rows, rows)
    out_specs = (rows, rows, P(ALL), rows, rows, P(ALL), rows, rows)
    return jax.shard_map(body, mesh=mesh, in_specs=in_specs, out_specs=out_specs, check_vma=False)
```

```python
import functools

import jax
import jax.numpy as jnp
import numpy as np
from jax import lax
from jax.experimental import pallas as pl
from jax.experimental.pallas import tpu as pltpu
from jax.sharding import PartitionSpec as P

HEADS = 32
HEAD_DIM = 64
THETA = 130000.0
EPS = 1e-05
TP = ("hs", "blk")
ALL = ("dp", "hs", "blk")
VMEM_LIMIT = 56 * 1024 * 1024
EXP2_SCALE = HEAD_DIM**-0.5 * 1.4426950408889634

F32 = jnp.float32
BF16 = jnp.bfloat16


def dot_nn(a, b):
    return lax.dot_general(a, b, (((1,), (0,)), ((), ())), preferred_element_type=F32)


def dot_nt(a, b):
    return lax.dot_general(a, b, (((1,), (1,)), ((), ())), preferred_element_type=F32)


def dot_tn(a, b):
    return lax.dot_general(a, b, (((0,), (0,)), ((), ())), preferred_element_type=F32)


def rms_scale(values, gain):
    return values * lax.rsqrt(jnp.mean(values * values, axis=-1, keepdims=True) + EPS) * gain


def rope_tables(blocks, block):
    half = HEAD_DIM // 2
    lane = np.arange(2 * HEAD_DIM)
    index = jnp.asarray(lane % half, F32)
    sign = jnp.asarray(np.where(lane % HEAD_DIM < half, -1.0, 1.0), F32)
    freq = jnp.power(F32(THETA), -2.0 * index / float(HEAD_DIM))[None, :]
    base = (jnp.arange(blocks, dtype=jnp.int32) * block).astype(F32)[:, None] * freq
    step = jnp.arange(block, dtype=jnp.int32).astype(F32)[:, None] * freq
    cos, sin = jnp.cos(step), jnp.sin(step)
    return (
        jnp.stack([jnp.cos(base), jnp.sin(base)]),
        jnp.stack([cos, sin, cos * sign, sin * sign]),
    )


def rope_of_block(base_ref, step_ref, b):
    cos, sin = base_ref[0, pl.ds(b, 1), :], base_ref[1, pl.ds(b, 1), :]
    return (
        cos * step_ref[0] - sin * step_ref[1],
        sin * step_ref[2] + cos * step_ref[3],
    )


def swap_halves(x):
    half = HEAD_DIM // 2
    width = x.shape[1]
    lane = lax.broadcasted_iota(jnp.int32, x.shape, 1)
    return jnp.where(
        lax.rem(lane, HEAD_DIM) < half,
        pltpu.roll(x, width - half, 1),
        pltpu.roll(x, half, 1),
    )


MESH = pl.DeviceIdType.MESH
CHUNKS = 2
FINE = 4


def position():
    z, b = lax.axis_index("hs"), lax.axis_index("blk")
    return z, b // 2, b % 2


def remote(src, dst, send, recv, **where):
    return pltpu.make_async_remote_copy(
        src_ref=src, dst_ref=dst, send_sem=send, recv_sem=recv, device_id=where, device_id_type=MESH
    )


def signal(sem, **where):
    pl.semaphore_signal(sem, inc=1, device_id=where, device_id_type=MESH)


def greet_neighbours(nz):
    z, y, c = position()
    barrier = pltpu.get_barrier_semaphore()
    signal(barrier, blk=y * 2 + 1 - c)
    signal(barrier, blk=(1 - y) * 2 + c)

    @pl.when(z > 0)
    def _():
        signal(barrier, hs=z - 1)

    @pl.when(z < nz - 1)
    def _():
        signal(barrier, hs=z + 1)

    count = 2 + jnp.where(z > 0, 1, 0) + jnp.where(z < nz - 1, 1, 0)
    pl.semaphore_wait(barrier, count)


def greet_all(nz, n_dp):
    z, y, c = position()
    peers = nz * 4
    me = z * 4 + y * 2 + c
    d = lax.axis_index("dp")
    barrier = pltpu.get_barrier_semaphore()

    @pl.loop(1, peers)
    def _(r):
        t = (me + r) % peers
        signal(barrier, hs=t // 4, blk=t % 4)

    @pl.loop(1, n_dp)
    def _(r):
        signal(barrier, dp=(d + r) % n_dp)

    pl.semaphore_wait(barrier, peers - 1 + n_dp - 1)


def by_distance(z, n, nz):
    near = jnp.minimum(z, nz - 1 - z)
    step = (n + 1) // 2
    both = jnp.where(n % 2 == 1, z - step, z + step)
    one = jnp.where(z < nz - 1 - z, n, nz - 1 - n)
    return jnp.where(n <= 2 * near, both, one)


def gather_sems(nz, chunks=CHUNKS):
    one, two = (nz, chunks), (nz, 2, chunks)
    return [pltpu.SemaphoreType.DMA(s) for s in (one, one, two, one, one, one, two)]


class Gather:
    def __init__(self, buf, sems, nz, lead=(), chunks=CHUNKS):
        self.buf, self.nz, self.lead, self.chunks = buf, nz, lead, chunks
        self.z, self.y, self.c = position()
        self.r_z, self.r_y, self.r_c, self.s_r, self.s_l, self.s_y, self.s_c = sems
        self.rows = buf.shape[-2] // chunks

    def part(self, zs, y, c, q):
        rows = pl.ds(pl.multiple_of(q * self.rows, self.rows), self.rows)
        return self.buf.at[(*self.lead, zs, y, c, rows, slice(None))]

    def right(self, zs, q):
        p = self.part(zs, self.y, self.c, q)
        return remote(p, p, self.s_r.at[zs, q], self.r_z.at[zs, q], hs=self.z + 1)

    def left(self, zs, q):
        p = self.part(zs, self.y, self.c, q)
        return remote(p, p, self.s_l.at[zs, q], self.r_z.at[zs, q], hs=self.z - 1)

    def across(self, zs, q):
        p = self.part(zs, self.y, self.c, q)
        return remote(
            p, p, self.s_y.at[zs, q], self.r_y.at[zs, q], blk=(1 - self.y) * 2 + self.c
        )

    def sibling(self, zs, y, q):
        p = self.part(zs, y, self.c, q)
        return remote(
            p, p, self.s_c.at[zs, y, q], self.r_c.at[zs, y, q], blk=self.y * 2 + 1 - self.c
        )

    def goes_right(self, zs):
        return jnp.logical_and(zs <= self.z, self.z < self.nz - 1)

    def goes_left(self, zs):
        return jnp.logical_and(zs >= self.z, self.z > 0)

    def row_part(self, n, q):
        zs = by_distance(self.z, n, self.nz)

        @pl.when(n > 0)
        def _():
            p = self.part(zs, self.y, self.c, q)
            remote(
                p, p, self.s_y.at[zs, q], self.r_z.at[zs, q], blk=self.y * 2 + 1 - self.c
            ).wait_recv()

        @pl.when(self.goes_right(zs))
        def _():
            self.right(zs, q).start()

        @pl.when(self.goes_left(zs))
        def _():
            self.left(zs, q).start()

        self.across(zs, q).start()
        self.sibling(zs, self.y, q).start()

    def cross_part(self, n, q):
        zs = by_distance(self.z, n, self.nz)
        p = self.part(zs, 1 - self.y, self.c, q)
        remote(
            p, p, self.s_y.at[zs, q], self.r_y.at[zs, q], blk=(1 - self.y) * 2 + self.c
        ).wait_recv()
        self.sibling(zs, 1 - self.y, q).start()

    def row_step(self, n):
        for q in range(self.chunks):
            self.row_part(n, q)

    def cross_step(self, n):
        for q in range(self.chunks):
            self.cross_part(n, q)

    def chunk_step(self, e):
        @pl.when(e < self.nz * self.chunks)
        def _():
            self.row_part(e // self.chunks, e % self.chunks)

        self.cross_part((e - self.chunks) // self.chunks, e % self.chunks)

    def ready(self, zs, y):
        for q in range(self.chunks):
            p = self.part(zs, y, 1 - self.c, q)
            remote(
                p, p, self.s_c.at[zs, y, q], self.r_c.at[zs, y, q], blk=self.y * 2 + 1 - self.c
            ).wait_recv()

    def drain(self):
        @pl.loop(0, self.nz)
        def _(zs):
            for q in range(self.chunks):

                @pl.when(self.goes_right(zs))
                def _():
                    self.right(zs, q).wait_send()

                @pl.when(self.goes_left(zs))
                def _():
                    self.left(zs, q).wait_send()

                self.across(zs, q).wait_send()
                self.sibling(zs, 0, q).wait_send()
                self.sibling(zs, 1, q).wait_send()


class DpGather:
    def __init__(self, buf, sems, nz, n_dp):
        self.d, self.n_dp, self.nz, self.buf = lax.axis_index("dp"), n_dp, nz, buf
        self.s_x, self.r_x, self.s_f, self.r_f = sems[:4]
        self.plane = Gather(buf, sems[4:], nz, (self.d,), 1)
        self.z, self.y, self.c = position()

    def to_dp(self, zs, y, r):
        p = self.buf.at[self.d, zs, y, self.c]
        sems = self.s_x.at[zs, y, r], self.r_x.at[zs, y, r]
        return remote(p, p, *sems, dp=(self.d + r) % self.n_dp)

    def relay(self, zs, y, c, r, sems):
        p = self.buf.at[(self.d + self.n_dp - r) % self.n_dp, zs, y, c]
        sems = (sem.at[zs, y, r] for sem in sems)
        return remote(p, p, *sems, blk=self.y * 2 + 1 - self.c)

    def row_step(self, n):
        self.plane.row_step(n)
        self.send_on(by_distance(self.z, n, self.nz), self.y)

    def cross_step(self, n):
        self.plane.cross_step(n)
        self.send_on(by_distance(self.z, n, self.nz), 1 - self.y)

    def send_on(self, zs, y):
        @pl.loop(1, self.n_dp)
        def _(r):
            self.to_dp(zs, y, r).start()

    def each(self, act):
        @pl.loop(0, self.nz)
        def _(n):
            zs = by_distance(self.z, n, self.nz)
            for y in (self.y, 1 - self.y):

                @pl.loop(1, self.n_dp)
                def _(r):
                    act(zs, y, r)

    def finish(self):
        def pass_on(zs, y, r):
            self.relay(zs, y, self.c, r, (self.s_x, self.r_x)).wait_recv()
            self.relay(zs, y, self.c, r, (self.s_f, self.r_f)).start()

        def end(zs, y, r):
            self.relay(zs, y, 1 - self.c, r, (self.s_f, self.r_f)).wait_recv()
            self.relay(zs, y, self.c, r, (self.s_f, self.r_f)).wait_send()
            self.to_dp(zs, y, r).wait_send()

        self.each(pass_on)

        @pl.loop(0, self.nz)
        def _(zs):
            self.plane.ready(zs, 0)
            self.plane.ready(zs, 1)

        self.each(end)
        self.plane.drain()


def dp_gather_sems(nz, n_dp):
    return [pltpu.SemaphoreType.DMA((nz, 2, n_dp)) for _ in range(4)] + gather_sems(nz, 1)


def scatter_sems(nz, chunks=CHUNKS):
    return [pltpu.SemaphoreType.DMA((nz * chunks,)) for _ in range(7)]


def scatter_buffers(nz, rows, width):
    two, one = pltpu.VMEM((nz, 2, rows, width), BF16), pltpu.VMEM((nz, rows, width), BF16)
    return [two, two, one, pltpu.VMEM((nz + 1, rows, width), BF16)]


class Scatter:
    def __init__(self, theirs, bufs, sems, nz, chunks=CHUNKS):
        self.theirs, self.nz, self.chunks = theirs, nz, chunks
        self.mine, self.rc, self.ry, self.rz = bufs
        self.s_c, self.r_c, self.s_y, self.r_y, self.s_z, self.r_l, self.r_r = sems
        self.z, self.y, self.c = position()
        self.rows = self.mine.shape[2] // chunks
        self.units = nz * chunks
        self.steps = self.units + nz + 1

    def place(self, k):
        r = k % (2 * self.chunks)
        pair = k // (2 * self.chunks)
        return jnp.where(r % 2 == 0, self.nz - 1 - pair, pair), r // 2

    def unit(self, k):
        zs, q = self.place(k)
        return zs, pl.ds(q * self.rows, self.rows)

    def to_sibling(self, k):
        zs, part = self.unit(k)
        return remote(
            self.theirs(zs, part), self.rc.at[zs, :, part, :], self.s_c.at[k], self.r_c.at[k],
            blk=self.y * 2 + 1 - self.c,
        )

    def across(self, k):
        zs, part = self.unit(k)
        return remote(
            self.mine.at[zs, 1 - self.y, part, :], self.ry.at[zs, part, :],
            self.s_y.at[k], self.r_y.at[k], blk=(1 - self.y) * 2 + self.c,
        )

    def right(self, k):
        zs, part = self.unit(k)
        return remote(
            self.mine.at[zs, self.y, part, :], self.rz.at[zs, part, :],
            self.s_z.at[k], self.r_l.at[k], hs=self.z + 1,
        )

    def left(self, k):
        zs, part = self.unit(k)
        place = jnp.where(zs == self.z - 1, self.nz, zs)
        return remote(
            self.mine.at[zs, self.y, part, :], self.rz.at[place, part, :],
            self.s_z.at[k], self.r_r.at[k], hs=self.z - 1,
        )

    def take(self, buf, sem, k, place=None):
        zs, part = self.unit(k)
        place = zs if place is None else place
        p = buf.at[place, part, :]
        remote(p, p, self.s_z.at[k], sem.at[k], blk=self.y * 2 + 1 - self.c).wait_recv()
        return buf[place, part, :].astype(F32)

    def add(self, k, row, other):
        zs, part = self.unit(k)
        self.mine[zs, row, part, :] = (self.mine[zs, row, part, :].astype(F32) + other).astype(
            BF16
        )

    def chip_sum(self, k):
        zs, part = self.unit(k)
        self.to_sibling(k).wait_recv()
        self.add(k, 1 - self.y, self.rc[zs, 1 - self.y, part, :].astype(F32))
        self.across(k).start()
        self.add(k, self.y, self.rc[zs, self.y, part, :].astype(F32))

    def row_sum(self, k):
        self.add(k, self.y, self.take(self.ry, self.r_y, k))

    def pass_on(self, k, buf, sem, start, first):
        @pl.when(jnp.logical_not(first))
        def _():
            self.add(k, self.y, self.take(buf, sem, k))

        start(k).start()

    def finish(self, k, out_ref):
        zs, part = self.unit(k)
        out_ref[part, :] = self.mine[zs, self.y, part, :].astype(F32)

        @pl.when(self.z > 0)
        def _():
            out_ref[part, :] += self.take(self.rz, self.r_l, k)

        @pl.when(self.z < self.nz - 1)
        def _():
            out_ref[part, :] += self.take(self.rz, self.r_r, k, self.nz)

    def later(self, k, out_ref):
        z, nz = self.z, self.nz

        def valid(m):
            return jnp.logical_and(m >= 0, m < self.units)

        @pl.when(valid(k - 1))
        def _():
            self.row_sum(k - 1)

        m = k - 1 - z

        @pl.when(jnp.logical_and(valid(m), self.unit(m)[0] > z))
        def _():
            self.pass_on(m, self.rz, self.r_l, self.right, z == 0)

        w = k - 1 - (nz - 1 - z)

        @pl.when(jnp.logical_and(valid(w), self.unit(w)[0] < z))
        def _():
            self.pass_on(w, self.rz, self.r_r, self.left, z == nz - 1)

        f = k - 1 - jnp.maximum(z, nz - 1 - z)

        @pl.when(jnp.logical_and(valid(f), self.unit(f)[0] == z))
        def _():
            self.finish(f, out_ref)

    def drain(self):
        @pl.loop(0, self.units)
        def _(k):
            self.to_sibling(k).wait_send()
            self.across(k).wait_send()

            @pl.when(self.unit(k)[0] > self.z)
            def _():
                self.right(k).wait_send()

            @pl.when(self.unit(k)[0] < self.z)
            def _():
                self.left(k).wait_send()


def exchange_sems(nz):
    dma = pltpu.SemaphoreType.DMA
    return [dma((nz * 4,)), dma((nz * 4,)), dma]


class Exchange:
    def __init__(self, src, dst, sems, nz):
        self.src, self.dst = src, dst
        self.send, self.recv, self.own = sems
        self.peers = nz * 4
        z, y, c = position()
        self.me = z * 4 + y * 2 + c

    def copy(self, r):
        t = (self.me + r) % self.peers
        return remote(
            self.src(t), self.dst(self.me), self.send.at[r], self.recv.at[r],
            hs=t // 4, blk=t % 4,
        )

    def arrival(self, r):
        t = (self.me + self.peers - r) % self.peers
        p = self.dst(t)
        return remote(p, p, self.send.at[r], self.recv.at[r], hs=t // 4, blk=t % 4)

    def keep(self):
        return pltpu.make_async_copy(self.src(self.me), self.dst(self.me), self.own)

    def start(self):
        self.keep().start()

        @pl.loop(1, self.peers)
        def _(r):
            self.copy(r).start()

    def arrive(self):
        self.keep().wait()

        @pl.loop(1, self.peers)
        def _(r):
            self.arrival(r).wait_recv()

    def drain(self):
        @pl.loop(1, self.peers)
        def _(r):
            self.copy(r).wait_send()


def outermost(i, nz):
    return jnp.where(i % 2 == 0, nz - 1 - i // 2, i // 2)


def early_blocks(peers):
    return peers // 4


def mlp_block_sems(nz, n_dp, count):
    dma = pltpu.SemaphoreType.DMA
    return [dma((count,)), dma((count, n_dp)), dma((count, n_dp))] + exchange_sems(nz)


class MlpBlocks:
    def __init__(self, parts, arrived, summed, out, sems, nz, n_dp, first, count):
        self.l_m, self.s_x, self.r_x = sems[:3]
        self.parts, self.arrived, self.summed, self.n_dp = parts, arrived, summed, n_dp
        self.peers = nz * 4
        self.first, self.last = first, first + count
        self.d = lax.axis_index("dp")
        self.moves = Exchange(
            lambda t: summed.at[(t - self.me + self.peers - 1) % self.peers + 1 - first],
            lambda t: out.at[t],
            sems[3:],
            nz,
        )
        self.me = self.moves.me

    def each(self, act):
        @pl.loop(self.first, self.last)
        def _(i):
            act(i)

    def each_dp(self, act):
        @pl.loop(1, self.n_dp)
        def _(r):
            act(r)

    def own(self, i):
        k = i - self.first
        t = (self.me + i) % self.peers
        return pltpu.make_async_copy(
            self.parts.at[self.d, t], self.summed.at[k], self.l_m.at[k]
        )

    def x_copy(self, i, r):
        k = i - self.first
        t = (self.me + i) % self.peers
        dp = (self.d + r) % self.n_dp
        return remote(
            self.parts.at[dp, t], self.arrived.at[r - 1, k],
            self.s_x.at[k, r], self.r_x.at[k, r], dp=dp,
        )

    def load(self):
        self.each(lambda i: self.own(i).start())

    def start(self):
        self.each(lambda i: self.each_dp(lambda r: self.x_copy(i, r).start()))

    def add(self, i):
        k = i - self.first
        self.own(i).wait()

        def one(r):
            self.x_copy(i, r).wait_recv()
            self.summed[k] = (
                self.summed[k].astype(F32) + self.arrived[r - 1, k].astype(F32)
            ).astype(BF16)

        self.each_dp(one)

        @pl.when(i < self.peers)
        def _():
            self.moves.copy(i).start()

        @pl.when(i == self.peers)
        def _():
            self.moves.keep().start()

    def finish(self):
        def end(i):
            @pl.when(i < self.peers)
            def _():
                self.moves.copy(i).wait_send()
                self.moves.arrival(i).wait_recv()

            @pl.when(i == self.peers)
            def _():
                self.moves.keep().wait()

            self.each_dp(lambda r: self.x_copy(i, r).wait_send())

        self.each(end)


def attn_fwd_kernel(
    nz, n_dp, block, tile, slot_ref, order_ref, qkv_ref, base_ref, step_ref, cot_ref, wm_ref,
    q_out, k_out, v_out, ctxt_out, lse_out, ctx_out, cot_all, wm_in,
    qm, vt, ctx_sorted, ctx_blocks, ctx_slots, g, own_sem, o_cot, s_x, r_x, *sems,
):
    gather = Gather(g, sems[3:], nz, chunks=FINE)
    z, y, c = gather.z, gather.y, gather.c
    d = lax.axis_index("dp")
    own = pltpu.make_async_copy(cot_ref, g.at[z, y, c], own_sem)
    own.start()

    def x_copy(r):
        return remote(
            wm_ref, wm_in.at[r - 1], s_x.at[r], r_x.at[r], dp=(d + r) % n_dp
        )

    def cot_copy(zs, yy):
        return pltpu.make_async_copy(g.at[zs, yy], cot_all.at[zs, yy], o_cot.at[zs, yy])
    moves = Exchange(
        lambda t: ctx_slots.at[t],
        lambda t: ctx_out.at[:, pl.ds(pl.multiple_of(t * 2 * HEAD_DIM, 128), 2 * HEAD_DIM)],
        sems[:3],
        nz,
    )
    greet_all(nz, n_dp)
    own.wait()
    gather.row_step(0)

    @pl.loop(1, n_dp)
    def _(r):
        x_copy(r).start()

    length = q_out.shape[0]
    width = 2 * HEAD_DIM
    n_blocks = length // block
    n_tiles = length // tile

    @pl.loop(0, n_blocks)
    def _(b):
        dst = pl.ds(pl.multiple_of(b * block, block), block)
        cos, sin = rope_of_block(base_ref, step_ref, b)
        qkv = qkv_ref[slot_ref[b]]
        q = qkv[:, 0:width]
        k = qkv[:, width : 2 * width]
        v = qkv[:, 2 * width : 3 * width]
        q = (q * cos + swap_halves(q) * sin).astype(BF16)
        k = (k * cos + swap_halves(k) * sin).astype(BF16)
        q_out[dst, :] = q
        k_out[dst, :] = k
        v_out[dst, :] = v.astype(BF16)
        low = lax.broadcasted_iota(jnp.int32, q.shape, 1) < HEAD_DIM
        zero = jnp.zeros_like(q)
        qm[0, dst, :] = jnp.where(low, q, zero)
        qm[1, dst, :] = jnp.where(low, zero, q)

    @pl.loop(0, n_tiles)
    def _(t):
        rows = pl.ds(pl.multiple_of(t * tile, tile), tile)
        both = v_out[rows, :].astype(F32).T.astype(BF16)
        for h in range(2):
            vt[h, 0:HEAD_DIM, rows] = both[h * HEAD_DIM : (h + 1) * HEAD_DIM, :]
            vt[h, HEAD_DIM:, rows] = jnp.ones((16, tile), BF16)

    diag = lax.broadcasted_iota(jnp.int32, (tile, tile), 0) <= lax.broadcasted_iota(
        jnp.int32, (tile, tile), 1
    )
    early = {6: [0], 5: [1], 4: [2], 3: [3], 2: [4, 5], 1: [6, 7]}
    early = {at: [FINE + e for e in events] for at, events in early.items()}

    @pl.loop(0, n_tiles)
    def _(i):
        rows_q = pl.ds(pl.multiple_of(i * tile, tile), tile)
        queries = [qm[0, rows_q, :], qm[1, rows_q, :]]

        def step(j, carry, masked):
            rows_k = pl.ds(pl.multiple_of(j * tile, tile), tile)
            keys = k_out[rows_k, :]
            new = []
            for h in range(2):
                top, acc = carry[h]
                s = dot_nt(keys, queries[h]) * EXP2_SCALE
                if masked:
                    s = jnp.where(diag, s, -1e30)
                new_top = jnp.maximum(top, jnp.max(s, axis=0, keepdims=True))
                p = jnp.exp2(s - new_top).astype(BF16)
                acc = acc * jnp.exp2(top - new_top) + dot_nn(vt[h, :, rows_k], p)
                new.append((new_top, acc))
            return tuple(new)

        start = tuple(
            (jnp.full((1, tile), -1e30, F32), jnp.zeros((HEAD_DIM + 16, tile), F32))
            for _ in range(2)
        )
        carry = lax.fori_loop(0, i, lambda j, c: step(j, c, False), start)
        carry = step(i, carry, True)
        outs = []
        for h in range(2):
            top, acc = carry[h]
            total = acc[HEAD_DIM : HEAD_DIM + 1, :]
            outs.append(acc[0:HEAD_DIM, :] / total)
            lse_out[h : h + 1, rows_q] = top + jnp.log2(total)
        both = jnp.concatenate(outs, axis=0)
        ctxt_out[:, rows_q] = both
        ctx_sorted[rows_q, :] = both.T.astype(BF16)

        for at, events in early.items():

            @pl.when(i == n_tiles - at)
            def _():
                for e in events:
                    gather.chunk_step(e)

    @pl.loop(0, n_blocks)
    def _(b):
        ctx_blocks[b] = ctx_sorted[pl.ds(pl.multiple_of(b * block, block), block), :]

    @pl.loop(0, n_blocks)
    def _(t):
        ctx_slots[t] = ctx_blocks[order_ref[t]]

    moves.start()

    @pl.loop(FINE + 8, nz * FINE + FINE)
    def _(e):
        gather.chunk_step(e)

    @pl.loop(0, nz)
    def _(n):
        zs = by_distance(z, n, nz)
        for yy in (y, 1 - y):
            gather.ready(zs, yy)
            cot_copy(zs, yy).start()

    moves.arrive()
    moves.drain()
    gather.drain()

    @pl.loop(0, nz)
    def _(zs):
        for yy in range(2):
            cot_copy(zs, yy).wait()

    @pl.loop(1, n_dp)
    def _(r):
        x_copy(r).wait()


def attn_fwd(slot_of_block, order, qkv, base, step, cot, wm, nz, n_dp, tile):
    length = qkv.shape[0]
    width = 2 * HEAD_DIM
    block, wide = cot.shape
    whole = pl.BlockSpec(memory_space=pltpu.VMEM)
    smem = pl.BlockSpec(memory_space=pltpu.SMEM)
    any_spec = pl.BlockSpec(memory_space=pl.ANY)
    *rest, cot_all, wm_in = pl.pallas_call(
        functools.partial(attn_fwd_kernel, nz, n_dp, block, tile),
        in_specs=[smem, smem, whole, whole, whole, any_spec, any_spec],
        out_specs=[whole] * 5 + [any_spec] * 3,
        out_shape=[
            jax.ShapeDtypeStruct((length, width), BF16),
            jax.ShapeDtypeStruct((length, width), BF16),
            jax.ShapeDtypeStruct((length, width), BF16),
            jax.ShapeDtypeStruct((width, length), F32),
            jax.ShapeDtypeStruct((2, length), F32),
            jax.ShapeDtypeStruct((block, wide), BF16),
            jax.ShapeDtypeStruct((nz, 2, 2, block, wide), BF16),
            jax.ShapeDtypeStruct((max(n_dp - 1, 1),) + wm.shape, BF16),
        ],
        scratch_shapes=[
            pltpu.VMEM((2, length, width), BF16),
            pltpu.VMEM((2, HEAD_DIM + 16, length), BF16),
            pltpu.VMEM((length, width), BF16),
            pltpu.VMEM((length // block, block, width), BF16),
            pltpu.VMEM((length // block, block, width), BF16),
            pltpu.VMEM((nz, 2, 2, block, wide), BF16),
            pltpu.SemaphoreType.DMA,
            pltpu.SemaphoreType.DMA((nz, 2)),
            pltpu.SemaphoreType.DMA((n_dp,)),
            pltpu.SemaphoreType.DMA((n_dp,)),
        ]
        + exchange_sems(nz)
        + gather_sems(nz, FINE),
        compiler_params=pltpu.CompilerParams(
            vmem_limit_bytes=VMEM_LIMIT, collective_id=5, has_side_effects=True
        ),
        cost_estimate=pl.CostEstimate(
            flops=20 * length * length * HEAD_DIM,
            bytes_accessed=30 * length * wide,
            transcendentals=length * length,
        ),
        name="attn_fwd",
    )(slot_of_block, order, qkv.reshape(length // block, block, -1), base, step, cot, wm)
    return *rest, cot_all.reshape(length, wide), wm_in


def attn_bwd_kernel(
    nz, n_dp, block, tile,
    slot_ref, order_ref, q_ref, k_ref, v_ref, dctx_ref, ctxt_ref, lse_ref, base_ref, step_ref, p_ref, go_ref, xn_ref, gm_ref,
    out_ref, sum_ref, go_in, gq_ref, gm_out,
    qm, dom, do_slots, do_sorted, kt, delta, dqt, dk_buf, dv_buf, d_blocks, acc, x_buf, gm_in, gm_sum,
    l_x, l_m, s_x, r_x, *rest,
):
    bufs, sems = rest[:4], rest[4:]
    sc = Scatter(lambda zs, part: p_ref.at[zs, :, 1 - sc.c, part, :], bufs, sems[9:], nz)
    n_early = early_blocks(nz * 4)
    mlp = MlpBlocks(gm_ref, gm_in, gm_sum, gm_out, sems[3:9], nz, n_dp, 1, n_early)
    moves = Exchange(
        lambda t: dctx_ref.at[:, pl.ds(pl.multiple_of(t * 2 * HEAD_DIM, 128), 2 * HEAD_DIM)],
        lambda t: do_slots.at[t],
        sems[:3],
        nz,
    )

    def load(k):
        zs, part = sc.unit(k)
        return pltpu.make_async_copy(
            p_ref.at[zs, :, sc.c, part, :], bufs[0].at[zs, :, part, :], l_m.at[k]
        )

    d = lax.axis_index("dp")

    def x_copy(i, r):
        t = (d + r) % n_dp
        zs = outermost(i, nz)
        return remote(go_ref.at[t, zs], go_in.at[r, zs], s_x.at[i, r], r_x.at[i, r], dp=t)

    mlp.load()
    greet_all(nz, n_dp)
    moves.start()
    mlp.start()

    @pl.loop(1, n_dp)
    def _(r):
        for i in range(nz - 1):
            x_copy(i, r).start()

    @pl.loop(0, sc.units)
    def _(k):
        sc.to_sibling(k).start()
        load(k).start()

    @pl.loop(0, sc.units)
    def _(k):
        load(k).wait()
        sc.chip_sum(k)

    for e in range(2):
        sc.later(1 + e, sum_ref)
        mlp.add(1 + e)
    moves.arrive()
    length = q_ref.shape[0]
    width = 2 * HEAD_DIM
    n_blocks = length // block
    n_tiles = length // tile
    scale = HEAD_DIM**-0.5

    @pl.loop(0, n_blocks)
    def _(b):
        dst = pl.ds(pl.multiple_of(b * block, block), block)
        do_sorted[dst, :] = do_slots[slot_ref[b]]

    @pl.loop(0, n_tiles)
    def _(t):
        rows = pl.ds(pl.multiple_of(t * tile, tile), tile)
        low = lax.broadcasted_iota(jnp.int32, (tile, width), 1) < HEAD_DIM
        q = q_ref[rows, :]
        do = do_sorted[rows, :]
        zero = jnp.zeros_like(q)
        qm[0, rows, :] = jnp.where(low, q, zero)
        qm[1, rows, :] = jnp.where(low, zero, q)
        dom[0, rows, :] = jnp.where(low, do, zero)
        dom[1, rows, :] = jnp.where(low, zero, do)
        kt[:, rows] = k_ref[rows, :].astype(F32).T.astype(BF16)
        prod = do.astype(F32).T * ctxt_ref[:, rows]
        delta[0:1, rows] = jnp.sum(prod[0:HEAD_DIM, :], axis=0, keepdims=True)
        delta[1:2, rows] = jnp.sum(prod[HEAD_DIM:, :], axis=0, keepdims=True)
        dqt[:, rows] = jnp.zeros((width, tile), F32)

    diag = lax.broadcasted_iota(jnp.int32, (tile, tile), 0) <= lax.broadcasted_iota(
        jnp.int32, (tile, tile), 1
    )

    @pl.loop(0, n_tiles)
    def _(j):
        sc.later(j + 3, sum_ref)

        @pl.when(j + 3 < mlp.last)
        def _():
            mlp.add(j + 3)

        rows_k = pl.ds(pl.multiple_of(j * tile, tile), tile)
        keys = k_ref[rows_k, :]
        vals = v_ref[rows_k, :]

        def step(i, carry, masked):
            rows_q = pl.ds(pl.multiple_of(i * tile, tile), tile)
            dk, dv = carry
            for h in range(2):
                s = dot_nt(keys, qm[h, rows_q, :]) * EXP2_SCALE
                p = jnp.exp2(s - lse_ref[h : h + 1, rows_q])
                if masked:
                    p = jnp.where(diag, p, 0.0)
                dp = dot_nt(vals, dom[h, rows_q, :])
                ds = (p * (dp - delta[h : h + 1, rows_q])).astype(BF16)
                dv = dv + dot_nn(p.astype(BF16), dom[h, rows_q, :])
                dk = dk + dot_nn(ds, qm[h, rows_q, :])
                part = slice(h * HEAD_DIM, (h + 1) * HEAD_DIM)
                dqt[part, rows_q] += dot_nn(kt[part, rows_k], ds)
            return dk, dv

        zero = jnp.zeros((tile, width), F32)
        carry = step(j, (zero, zero), True)
        dk, dv = lax.fori_loop(j + 1, n_tiles, lambda i, c: step(i, c, False), carry)
        dk_buf[rows_k, :] = (dk * scale).astype(BF16)
        dv_buf[rows_k, :] = dv.astype(BF16)

    @pl.loop(0, n_tiles)
    def _(t):
        rows = pl.ds(pl.multiple_of(t * tile, tile), tile)
        do_sorted[rows, :] = (dqt[:, rows].T * scale).astype(BF16)

    @pl.loop(0, n_blocks)
    def _(b):
        src = pl.ds(pl.multiple_of(b * block, block), block)
        cos, sin = rope_of_block(base_ref, step_ref, b)
        dq = do_sorted[src, :].astype(F32)
        dk = dk_buf[src, :].astype(F32)
        d_blocks[b, :, 0:width] = (dq * cos - swap_halves(dq) * sin).astype(BF16)
        d_blocks[b, :, width : 2 * width] = (dk * cos - swap_halves(dk) * sin).astype(BF16)
        d_blocks[b, :, 2 * width : 3 * width] = dv_buf[src, :]

    @pl.loop(0, n_blocks)
    def _(t):
        out_ref[t] = d_blocks[order_ref[t]]

    def x_load(p):
        return pltpu.make_async_copy(xn_ref.at[p], x_buf.at[p % 2], l_x.at[p % 2])

    pairs = xn_ref.shape[0]
    x_load(0).start()
    acc[...] = jnp.zeros_like(acc)

    first = n_tiles + 3

    @pl.loop(0, max(sc.steps - first, pairs))
    def _(p):
        @pl.when(p < pairs)
        def _():
            @pl.when(p + 1 < pairs)
            def _():
                x_load(p + 1).start()

            x_load(p).wait()
            d_pair = out_ref[pl.ds(2 * p, 2)].reshape(2 * block, 3 * width)
            acc[...] += dot_tn(x_buf[p % 2], d_pair)

        @pl.when(first + p < sc.steps)
        def _():
            sc.later(first + p, sum_ref)

    gq_ref[...] = acc[...].astype(BF16)
    moves.drain()
    sc.drain()
    mlp.finish()

    @pl.loop(1, n_dp)
    def _(r):
        for i in range(nz - 1):
            x_copy(i, r).wait()


def attn_bwd(
    slot_of_block, order, q, k, v, d_ctx, ctxt, lse, base, step, partial, grad_out, xn, grad_mlp, nz, tile
):
    length, width = q.shape
    block, wide = d_ctx.shape
    whole = pl.BlockSpec(memory_space=pltpu.VMEM)
    smem = pl.BlockSpec(memory_space=pltpu.SMEM)
    any_spec = pl.BlockSpec(memory_space=pl.ANY)
    n_dp, peers, shard, cols_mlp = grad_mlp.shape
    d_qkv, summed, grad_out_in, grad_qkv, grad_mlp = pl.pallas_call(
        functools.partial(attn_bwd_kernel, nz, n_dp, block, tile),
        in_specs=[smem, smem] + [whole] * 3 + [any_spec] + [whole] * 4 + [any_spec] * 4,
        out_specs=[whole, whole, any_spec, whole, any_spec],
        out_shape=[
            jax.ShapeDtypeStruct((length // block, block, 3 * width), BF16),
            jax.ShapeDtypeStruct((block, wide), F32),
            jax.ShapeDtypeStruct(grad_out.shape, BF16),
            jax.ShapeDtypeStruct((wide, 3 * width), BF16),
            jax.ShapeDtypeStruct((peers, shard, cols_mlp), BF16),
        ],
        scratch_shapes=[
            pltpu.VMEM((2, length, width), BF16),
            pltpu.VMEM((2, length, width), BF16),
            pltpu.VMEM((length // block, block, width), BF16),
            pltpu.VMEM((length, width), BF16),
            pltpu.VMEM((width, length), BF16),
            pltpu.VMEM((2, length), F32),
            pltpu.VMEM((width, length), F32),
            pltpu.VMEM((length, width), BF16),
            pltpu.VMEM((length, width), BF16),
            pltpu.VMEM((length // block, block, 3 * width), BF16),
            pltpu.VMEM((wide, 3 * width), F32),
            pltpu.VMEM((2, 2 * block, wide), BF16),
            pltpu.VMEM((n_dp - 1, early_blocks(peers), shard, cols_mlp), BF16),
            pltpu.VMEM((early_blocks(peers), shard, cols_mlp), BF16),
            pltpu.SemaphoreType.DMA((2,)),
            pltpu.SemaphoreType.DMA((nz * CHUNKS,)),
            pltpu.SemaphoreType.DMA((nz - 1, n_dp)),
            pltpu.SemaphoreType.DMA((nz - 1, n_dp)),
        ]
        + scatter_buffers(nz, block, wide)
        + exchange_sems(nz)
        + mlp_block_sems(nz, n_dp, early_blocks(peers))
        + scatter_sems(nz),
        compiler_params=pltpu.CompilerParams(
            vmem_limit_bytes=VMEM_LIMIT, collective_id=6, has_side_effects=True
        ),
        cost_estimate=pl.CostEstimate(
            flops=50 * length * length * HEAD_DIM,
            bytes_accessed=60 * length * wide,
            transcendentals=length * length,
        ),
        name="attn_bwd",
    )(
        slot_of_block, order, q, k, v, d_ctx, ctxt, lse, base, step,
        partial.reshape(nz, 2, 2, block, wide), grad_out,
        xn.reshape(2 * nz, 2 * block, wide), grad_mlp,
    )
    return d_qkv.reshape(length, 3 * width), summed, grad_out_in, grad_qkv, grad_mlp


def scatter_mlp_kernel(
    nz, p_ref, x_ref, c_ref, dgu_ref, hid_ref,
    out_ref, grad_ref,
    acc, x_buf, c_buf, dgu_buf, hid_buf, l_m, l_x, l_c, l_g, l_h, *rest,
):
    bufs, sems = rest[:4], rest[4:]
    mine = bufs[0]
    pairs = x_ref.shape[0]
    gate_up = dgu_ref.shape[2]
    tile = 512 if acc.shape[0] % 512 == 0 else acc.shape[0]

    sc = Scatter(lambda zs, part: p_ref.at[zs, :, 1 - sc.c, part, :], bufs, sems, nz)

    def load(k):
        zs, part = sc.unit(k)
        return pltpu.make_async_copy(
            p_ref.at[zs, :, sc.c, part, :], mine.at[zs, :, part, :], l_m.at[k]
        )

    def operands(k):
        s = k % 2
        return [
            pltpu.make_async_copy(ref.at[k], buf.at[s], sem.at[s])
            for ref, buf, sem in (
                (x_ref, x_buf, l_x),
                (c_ref, c_buf, l_c),
                (dgu_ref, dgu_buf, l_g),
                (hid_ref, hid_buf, l_h),
            )
        ]

    every = sc.units // pairs
    greet_neighbours(nz)

    @pl.loop(0, sc.units)
    def _(k):
        sc.to_sibling(k).start()
        load(k).start()

    for copy in operands(0):
        copy.start()
    acc[...] = jnp.zeros_like(acc)

    def weight_grads(k):
        @pl.when(k + 1 < pairs)
        def _():
            for copy in operands(k + 1):
                copy.start()

        for copy in operands(k):
            copy.wait()
        s = k % 2

        @pl.loop(0, acc.shape[0] // tile)
        def _(t):
            at = pl.ds(pl.multiple_of(t * tile, tile), tile)
            acc[at, 0:gate_up] += dot_tn(x_buf[s, :, at], dgu_buf[s])
            acc[at, gate_up:] += dot_tn(c_buf[s, :, at], hid_buf[s])

    def chip_sum(k):
        load(k).wait()
        sc.chip_sum(k)

    for k in range(2):
        chip_sum(k)

    @pl.loop(0, sc.steps)
    def _(k):
        @pl.when(k + 2 < sc.units)
        def _():
            chip_sum(k + 2)

        sc.later(k, out_ref)

        @pl.when(jnp.logical_and(k % every == 0, k // every < pairs))
        def _():
            weight_grads(k // every)

    grad_ref[...] = acc[...].astype(BF16)
    sc.drain()


def scatter_mlp(partial, x_all, c_all, d_gu, hid, nz, collective_id):
    rows, width = partial.shape[0] // (nz * 4), partial.shape[1]
    hidden = hid.shape[1]
    pairs = 2 * nz
    any_spec = pl.BlockSpec(memory_space=pl.ANY)
    vmem = pl.BlockSpec(memory_space=pltpu.VMEM)
    dma = pltpu.SemaphoreType.DMA

    def by_pair(a):
        return a.reshape(pairs, 2 * rows, a.shape[1])

    def buffers(cols):
        return pltpu.VMEM((2, 2 * rows, cols), BF16)

    return pl.pallas_call(
        functools.partial(scatter_mlp_kernel, nz),
        in_specs=[any_spec] * 5,
        out_specs=[vmem, vmem],
        out_shape=[
            jax.ShapeDtypeStruct((rows, width), F32),
            jax.ShapeDtypeStruct((width, 3 * hidden), BF16),
        ],
        scratch_shapes=[
            pltpu.VMEM((width, 3 * hidden), F32),
            buffers(width),
            buffers(width),
            buffers(2 * hidden),
            buffers(hidden),
            dma((nz * CHUNKS,)),
            dma((2,)),
            dma((2,)),
            dma((2,)),
            dma((2,)),
        ]
        + scatter_buffers(nz, rows, width)
        + scatter_sems(nz),
        compiler_params=pltpu.CompilerParams(
            vmem_limit_bytes=VMEM_LIMIT, collective_id=collective_id, has_side_effects=True
        ),
        cost_estimate=pl.CostEstimate(
            flops=6 * partial.size * hidden,
            bytes_accessed=60 * partial.size,
            transcendentals=0,
        ),
        name="scatter_mlp",
    )(
        partial.reshape(nz, 2, 2, rows, width),
        by_pair(x_all),
        by_pair(c_all),
        by_pair(d_gu),
        by_pair(hid),
    )


def scatter_last_kernel(
    nz, n_dp, dq_ref, w_ref, gq_ref, gm_ref, go_ref, go_in,
    out_ref, gq_out, gm_out,
    theirs, gq_in, gq_sum, gm_in, gm_sum, go_buf, go_early,
    l_o, s_xo, r_xo, l_q, s_xq, r_xq, *rest,
):
    bufs, sems = rest[:4], rest[4:]
    sc = Scatter(lambda zs, part: theirs.at[zs, :, part, :], bufs, sems[9:], nz, FINE)
    mine = bufs[0]
    d = lax.axis_index("dp")
    rows, width = dq_ref.shape[3], mine.shape[3]
    shard = gq_in.shape[2]
    cols = dq_ref.shape[4]
    gq_moves = Exchange(lambda t: gq_sum.at[t], lambda t: gq_out.at[t], sems[:3], nz)
    n_early = early_blocks(nz * 4)
    mlp = MlpBlocks(
        gm_ref, gm_in, gm_sum, gm_out, sems[3:9], nz, n_dp, 1 + n_early, nz * 4 - n_early
    )
    keep_q = pltpu.make_async_copy(gq_ref.at[d], gq_in.at[0], l_q)
    keep_q.start()
    mlp.load()

    def xq_copy(r):
        t = (d + r) % n_dp
        return remote(gq_ref.at[t], gq_in.at[r], s_xq.at[r], r_xq.at[r], dp=t)

    def xo_copy(r):
        t = (d + r) % n_dp
        zs = outermost(nz - 1, nz)
        return remote(go_ref.at[t, zs], go_buf.at[r], s_xo.at[r], r_xo.at[r], dp=t)

    greet_all(nz, n_dp)

    @pl.loop(1, n_dp)
    def _(r):
        xq_copy(r).start()
        xo_copy(r).start()

    mlp.start()

    def partial_sums(zs, core):
        left = dq_ref[zs, :, core].reshape(2 * rows, cols)
        return dot_nt(left, w_ref[:, 0:cols]).astype(BF16).reshape(2, rows, width)

    def out_loads(zs, last):
        own = pltpu.make_async_copy(go_ref.at[d, zs], buf_of(last).at[0], l_o.at[0])
        return [own] + [
            xo_copy(r)
            if last
            else pltpu.make_async_copy(go_in.at[r, zs], go_early.at[r], l_o.at[r])
            for r in range(1, n_dp)
        ]

    def buf_of(last):
        return go_buf if last else go_early

    def out_sums(core, last):
        return sum(buf_of(last)[r, :, core].astype(F32) for r in range(n_dp)).astype(BF16)

    if mine.shape[2] > rows + shard:
        for buf in (mine, theirs):
            buf[:, :, rows + shard :, :] = jnp.zeros_like(buf[:, :, rows + shard :, :])

    def produce(i, last):
        zs = outermost(i, nz)
        loads = out_loads(zs, last)
        loads[0].start()
        if not last:
            for copy in loads[1:]:
                copy.start()
        theirs[zs, :, 0:rows, :] = partial_sums(zs, 1 - sc.c)
        loads[0].wait()
        for copy in loads[1:]:
            if last:
                copy.wait_recv()
            else:
                copy.wait()
        theirs[zs, :, rows : rows + shard, :] = out_sums(1 - sc.c, last)
        for q in range(FINE):
            sc.to_sibling(2 * FINE * (i // 2) + 2 * q + i % 2).start()
        mine[zs, :, 0:rows, :] = partial_sums(zs, sc.c)
        mine[zs, :, rows : rows + shard, :] = out_sums(sc.c, last)

    @pl.loop(0, 2)
    def _(i):
        produce(i, False)

    @pl.loop(0, 2)
    def _(i):
        sc.chip_sum(i)

    @pl.loop(0, sc.steps)
    def _(k):
        @pl.when(k + 2 < sc.units)
        def _():
            sc.chip_sum(k + 2)

        sc.later(k, out_ref)

        @pl.when(jnp.logical_and(k >= 1, k < nz - 2))
        def _():
            produce(k + 1, False)

        @pl.when(k == nz + 1)
        def _():
            produce(nz - 1, True)

        @pl.when(k == 1)
        def _():
            keep_q.wait()
            gq_sum[...] = gq_in[0]

            @pl.loop(1, n_dp)
            def _(r):
                xq_copy(r).wait_recv()
                gq_sum[...] = (gq_sum[...].astype(F32) + gq_in[r].astype(F32)).astype(BF16)

            gq_moves.start()

        i = mlp.first + k - 7

        @pl.when(jnp.logical_and(i >= mlp.first, i < mlp.last))
        def _():
            mlp.add(i)

    sc.drain()
    gq_moves.arrive()
    gq_moves.drain()
    mlp.finish()

    @pl.loop(1, n_dp)
    def _(r):
        xq_copy(r).wait_send()
        xo_copy(r).wait_send()


def scatter_last(d_qkv, w, grad_qkv, grad_mlp, grad_out, grad_out_in, nz, n_dp, collective_id):
    peers = nz * 4
    rows, cols = d_qkv.shape[0] // peers, d_qkv.shape[1]
    width = w.shape[0]
    shard = width // (n_dp * peers)
    cols_mlp = grad_mlp.shape[3]
    all_rows = rows + max(shard, 16 * FINE)
    any_spec = pl.BlockSpec(memory_space=pl.ANY)
    vmem = pl.BlockSpec(memory_space=pltpu.VMEM)
    dma = pltpu.SemaphoreType.DMA
    return pl.pallas_call(
        functools.partial(scatter_last_kernel, nz, n_dp),
        in_specs=[vmem, vmem] + [any_spec] * 4,
        out_specs=[vmem, any_spec, any_spec],
        out_shape=[
            jax.ShapeDtypeStruct((all_rows, width), F32),
            jax.ShapeDtypeStruct((peers, shard, cols), BF16),
            jax.ShapeDtypeStruct((peers, shard, cols_mlp), BF16),
        ],
        scratch_shapes=[
            pltpu.VMEM((nz, 2, all_rows, width), BF16),
            pltpu.VMEM((n_dp, peers, shard, cols), BF16),
            pltpu.VMEM((peers, shard, cols), BF16),
            pltpu.VMEM((n_dp - 1, peers - early_blocks(peers), shard, cols_mlp), BF16),
            pltpu.VMEM((peers - early_blocks(peers), shard, cols_mlp), BF16),
            pltpu.VMEM((n_dp, 2, 2, shard, width), BF16),
            pltpu.VMEM((n_dp, 2, 2, shard, width), BF16),
            dma((n_dp,)),
            dma((n_dp,)),
            dma((n_dp,)),
            dma,
            dma((n_dp,)),
            dma((n_dp,)),
        ]
        + scatter_buffers(nz, all_rows, width)
        + exchange_sems(nz)
        + mlp_block_sems(nz, n_dp, peers - early_blocks(peers))
        + scatter_sems(nz, FINE),
        compiler_params=pltpu.CompilerParams(
            vmem_limit_bytes=VMEM_LIMIT, collective_id=collective_id, has_side_effects=True
        ),
        cost_estimate=pl.CostEstimate(
            flops=2 * peers * rows * width * cols,
            bytes_accessed=60 * peers * rows * width,
            transcendentals=0,
        ),
        name="scatter_last",
    )(
        d_qkv.reshape(nz, 2, 2, rows, cols),
        w,
        grad_qkv.reshape(n_dp, peers, shard, cols),
        grad_mlp,
        grad_out.reshape(n_dp, nz, 2, 2, shard, width),
        grad_out_in.reshape(n_dp, nz, 2, 2, shard, width),
    )


def layout_kernel(
    gq_ref, gm_early, gm_late, wq_ref, wgu_ref, g1_ref, g2_ref, sum_ref, x_ref, gain_ref, dmid_ref, y_ref, mlp_ref,
    q_out, gu_out, down_out, g1_out, g2_out, layer_out, tok_out, wout_out,
):
    rows = x_ref.shape[0]
    layer_out[...] = (y_ref[...] + mlp_ref[...]).astype(BF16)
    wout_out[...] = sum_ref[rows : rows + wout_out.shape[0], :]
    x = x_ref[...].astype(F32)
    scaled = sum_ref[0:rows, :] * gain_ref[0:1, :]
    inverse = lax.rsqrt(jnp.mean(x * x, axis=1, keepdims=True) + EPS)
    along = jnp.mean(scaled * x, axis=1, keepdims=True) * (inverse * inverse)
    tok_out[...] = dmid_ref[...] + inverse * (scaled - x * along)

    peers = gq_ref.shape[0]
    part_q = gq_ref.shape[2] // 3
    hid = gm_early.shape[2] // 3
    z, y, c = position()
    me = z * 4 + y * 2 + c
    sum_q = jnp.zeros((gq_ref.shape[1], part_q), F32)
    sum_m = jnp.zeros((gq_ref.shape[1], hid), F32)
    for t in range(peers):
        for s in range(3):
            at = pl.ds((s * peers + t) * part_q, part_q)
            block = gq_ref[t, :, s * part_q : (s + 1) * part_q].astype(F32)
            q_out[:, at] = block
            sum_q += block * wq_ref[:, at].astype(F32)
        far = (me - t + peers - 1) % peers + 1
        from_t = jnp.where(far <= early_blocks(peers), gm_early[t], gm_late[t]).astype(F32)
        for s in range(2):
            at = pl.ds((s * peers + t) * hid, hid)
            block = from_t[:, s * hid : (s + 1) * hid]
            gu_out[:, at] = block
            sum_m += block * wgu_ref[:, at].astype(F32)
        down_out[:, t * hid : (t + 1) * hid] = from_t[:, 2 * hid :]

    def as_row(sums):
        column = jnp.sum(sums, axis=1, keepdims=True)
        return jnp.broadcast_to(column, (column.shape[0], 128)).T[0:1, :]

    g1_out[...] = as_row(sum_q) / g1_ref[...].astype(F32)
    g2_out[...] = as_row(sum_m) / g2_ref[...].astype(F32)


def layout_call(
    grad_qkv, mlp_early, mlp_late, w_qkv, w_gate_up, gain_one, gain_two, sums, tokens, gains, d_mid, y_mid, mlp_out
):
    shard = w_qkv.shape[0]
    hidden = w_gate_up.shape[1] // 2
    vmem = pl.BlockSpec(memory_space=pltpu.VMEM)
    return pl.pallas_call(
        layout_kernel,
        in_specs=[vmem] * 13,
        out_specs=[vmem] * 8,
        out_shape=[
            jax.ShapeDtypeStruct(w_qkv.shape, F32),
            jax.ShapeDtypeStruct(w_gate_up.shape, F32),
            jax.ShapeDtypeStruct((shard, hidden), F32),
            jax.ShapeDtypeStruct((1, shard), F32),
            jax.ShapeDtypeStruct((1, shard), F32),
            jax.ShapeDtypeStruct(tokens.shape, BF16),
            jax.ShapeDtypeStruct(tokens.shape, F32),
            jax.ShapeDtypeStruct((shard, tokens.shape[1]), F32),
        ],
        compiler_params=pltpu.CompilerParams(vmem_limit_bytes=VMEM_LIMIT),
        name="layout",
    )(
        grad_qkv, mlp_early, mlp_late, w_qkv, w_gate_up, gain_one[None], gain_two[None],
        sums, tokens, gains, d_mid, y_mid, mlp_out,
    )


def gather_qkv_kernel(
    nz, n_dp, tok_ref, wq_ref, wgu_ref, wd_ref, wo_ref,
    xn_ref, qkv_ref, gain_ref, wq_out, wm_out, wo_out,
    g, wq, xn_stage, own_sem, s_w, r_w, s_d, r_d, s_m, r_m, own_w, own_m, own_o, o_xn, o_w,
    *sems,
):
    peers = nz * 4
    gather = Gather(g, sems[:7], nz)
    w_out = DpGather(wo_out, sems[7:], nz, n_dp)
    z, y, c = gather.z, gather.y, gather.c
    me = z * 4 + y * 2 + c
    d = lax.axis_index("dp")
    pair_rows = 2 * tok_ref.shape[0]
    cols = qkv_ref.shape[2]
    shard = wq_ref.shape[1]
    hid = wd_ref.shape[1] // peers

    def block_rows(dp, t):
        return pl.ds(pl.multiple_of((dp * peers + t) * shard, shard), shard)

    def plane_rows(dp):
        return pl.ds(pl.multiple_of(dp * (peers * shard), peers * shard), peers * shard)

    def mlp_part(t, s):
        first = t * hid if s != 1 else (peers + t) * hid
        cols_t = pl.ds(pl.multiple_of(first, hid), hid)
        return (wd_ref if s == 2 else wgu_ref).at[:, cols_t]

    def mlp_place(t, s):
        return wm_out.at[block_rows(0, t), pl.ds(s * hid, hid)]

    own = pltpu.make_async_copy(tok_ref, g.at[z, y, c], own_sem)
    own.start()
    keep_w = pltpu.make_async_copy(wq_ref.at[me], wq.at[block_rows(d, me), :], own_w)
    keep_w.start()
    keep_o = pltpu.make_async_copy(wo_ref, wo_out.at[d, z, y, c], own_o)
    keep_o.start()
    keep_m = [
        pltpu.make_async_copy(mlp_part(me, s), mlp_place(me, s), own_m.at[s]) for s in range(3)
    ]
    for copy in keep_m:
        copy.start()

    greet_all(nz, n_dp)

    def place(t):
        return {"hs": t // 4, "blk": t % 4}

    def w_copy(r):
        t = (me + r) % peers
        return remote(
            wq_ref.at[t], wq.at[block_rows(d, me), :], s_w.at[r], r_w.at[r], **place(t)
        )

    def w_take(r):
        t = (me + peers - r) % peers
        p = wq.at[block_rows(d, t), :]
        return remote(p, p, s_w.at[r], r_w.at[r], **place(t))

    def m_copy(r, s):
        t = (me + r) % peers
        return remote(
            mlp_part(t, s), mlp_place(me, s), s_m.at[r, s], r_m.at[r, s], **place(t)
        )

    def m_take(r, s):
        t = (me + peers - r) % peers
        p = mlp_place(t, s)
        return remote(p, p, s_m.at[r, s], r_m.at[r, s], **place(t))

    def d_copy(r):
        p = wq.at[plane_rows(d), :]
        return remote(p, p, s_d.at[r], r_d.at[r], dp=(d + r) % n_dp)

    def d_take(r):
        p = wq.at[plane_rows((d + n_dp - r) % n_dp), :]
        return remote(p, p, s_d.at[r], r_d.at[r], dp=(d + r) % n_dp)

    def mlp_sends(first, last):
        @pl.loop(first, last)
        def _(r):
            for s in range(3):
                m_copy(r, s).start()

    own.wait()
    gather.row_step(0)

    @pl.loop(1, peers)
    def _(r):
        w_copy(r).start()

    keep_o.wait()
    w_out.row_step(0)
    third = peers // 3
    mlp_sends(1, 1 + third)
    gather.row_step(1)
    gather.cross_step(0)
    mlp_sends(1 + third, 1 + 2 * third)
    w_out.row_step(1)
    w_out.cross_step(0)

    @pl.loop(1, peers)
    def _(r):
        w_take(r).wait_recv()

    keep_w.wait()

    @pl.loop(1, n_dp)
    def _(r):
        d_copy(r).start()

    @pl.loop(2, nz)
    def _(n):
        gather.row_step(n)
        gather.cross_step(n - 1)

        @pl.when(n == 2)
        def _():
            mlp_sends(1 + 2 * third, peers)

        w_out.row_step(n)
        w_out.cross_step(n - 1)

    @pl.loop(1, n_dp)
    def _(r):
        d_take(r).wait_recv()

    gain_ref[...] = wq[:, cols:].astype(F32).T[0:8, :]
    keep_out = pltpu.make_async_copy(wq, wq_out, o_w)
    keep_out.start()
    gain = gain_ref[0:1, :]

    def xn_copy(m, pair):
        return pltpu.make_async_copy(xn_stage.at[m % 2], xn_ref.at[pair], o_xn.at[m % 2])

    @pl.loop(0, 2 * nz)
    def _(m):
        zs = by_distance(z, m // 2, nz)
        yy = jnp.where(m % 2 == 0, y, 1 - y)
        pair = zs * 2 + yy

        @pl.when(m == 2 * nz - 1)
        def _():
            gather.cross_step(nz - 1)
            w_out.cross_step(nz - 1)

        gather.ready(zs, yy)

        @pl.when(m >= 2)
        def _():
            xn_copy(m, pair).wait()

        x = g[zs, yy].reshape(pair_rows, g.shape[4]).astype(F32)
        xn = rms_scale(x, gain).astype(BF16)
        xn_stage[m % 2] = xn
        xn_copy(m, pair).start()
        qkv_ref[pair] = dot_nn(xn, wq[:, 0:cols])

    w_out.finish()
    for m in range(2):
        xn_copy(m, 0).wait()
    gather.drain()
    keep_out.wait()

    @pl.loop(1, peers)
    def _(r):
        w_copy(r).wait_send()
        for s in range(3):
            m_copy(r, s).wait_send()
            m_take(r, s).wait_recv()

    for copy in keep_m:
        copy.wait()

    @pl.loop(1, n_dp)
    def _(r):
        d_copy(r).wait_send()


def gather_qkv(tokens, wq_parts, w_gate_up, w_down, w_out, nz, n_dp, cols):
    rows, width = tokens.shape
    peers, shard, wide = wq_parts.shape
    hid = w_down.shape[1] // peers
    any_spec = pl.BlockSpec(memory_space=pl.ANY)
    vmem = pl.BlockSpec(memory_space=pltpu.VMEM)
    dma = pltpu.SemaphoreType.DMA
    length = peers * rows
    xn, qkv, gains, wq, wm, wo = pl.pallas_call(
        functools.partial(gather_qkv_kernel, nz, n_dp),
        in_specs=[any_spec] * 5,
        out_specs=[any_spec, vmem, vmem, any_spec, any_spec, any_spec],
        out_shape=[
            jax.ShapeDtypeStruct((peers // 2, 2 * rows, width), BF16),
            jax.ShapeDtypeStruct((peers // 2, 2 * rows, cols), F32),
            jax.ShapeDtypeStruct((8, width), F32),
            jax.ShapeDtypeStruct((width, wide), BF16),
            jax.ShapeDtypeStruct((width // n_dp, 3 * hid), BF16),
            jax.ShapeDtypeStruct((n_dp, nz, 2, 2, shard, width), BF16),
        ],
        scratch_shapes=[
            pltpu.VMEM((nz, 2, 2, rows, width), BF16),
            pltpu.VMEM((n_dp * peers * shard, wide), BF16),
            pltpu.VMEM((2, 2 * rows, width), BF16),
            dma,
            dma((peers,)),
            dma((peers,)),
            dma((n_dp,)),
            dma((n_dp,)),
            dma((peers, 3)),
            dma((peers, 3)),
            dma,
            dma((3,)),
            dma,
            dma((2,)),
            dma,
        ]
        + gather_sems(nz)
        + dp_gather_sems(nz, n_dp),
        compiler_params=pltpu.CompilerParams(
            vmem_limit_bytes=VMEM_LIMIT, collective_id=1, has_side_effects=True
        ),
        cost_estimate=pl.CostEstimate(
            flops=2 * length * width * cols,
            bytes_accessed=60 * length * width,
            transcendentals=0,
        ),
        name="gather_qkv",
    )(tokens, wq_parts, w_gate_up, w_down, w_out)
    return (
        xn.reshape(length, width), qkv.reshape(length, cols), gains, wq, wm,
        wo.reshape(width, width),
    )


def gather_mlp_kernel(
    nz, n_dp, x_ref, c_ref, wm_ref, wm_in,
    xn_ref, out_ref, dx_ref, hid_ref, dgu_ref,
    g, w_ref, c_buf, out_buf, dx_buf, hid_buf, dgu_buf,
    w_sem, own_sem, c_sem, x_sem, out_sem, dx_sem, hid_sem, dgu_sem, *sems,
):
    gather = Gather(g, sems, nz)
    z, y, c = gather.z, gather.y, gather.c
    hidden = w_ref.shape[1] // 3
    w_gate, w_up, w_down = (pl.ds(i * hidden, hidden) for i in range(3))
    pair_rows = 2 * x_ref.shape[0]
    steps = 2 * nz

    own = pltpu.make_async_copy(x_ref, g.at[z, y, c], own_sem)
    own.start()
    d = lax.axis_index("dp")
    half = wm_ref.shape[0]

    def w_load(r):
        start = pl.multiple_of(((d + n_dp - r) % n_dp) * half, half)
        src = wm_ref if r == 0 else wm_in.at[r - 1]
        return pltpu.make_async_copy(src, w_ref.at[pl.ds(start, half), :], w_sem.at[r])

    for r in range(n_dp):
        w_load(r).start()

    def place(m):
        return by_distance(z, m // 2, nz), jnp.where(m % 2 == 0, y, 1 - y)

    def pair(m):
        zs, yy = place(m)
        return zs * 2 + yy

    def c_copy(m):
        return pltpu.make_async_copy(c_ref.at[pair(m)], c_buf.at[m % 2], c_sem.at[m % 2])

    def x_copy(m):
        zs, yy = place(m)
        return pltpu.make_async_copy(g.at[zs, yy], xn_ref.at[zs, yy], x_sem.at[m])

    def results(m):
        s = m % 2
        return [
            pltpu.make_async_copy(buf.at[s], ref.at[pair(m)], sem.at[s])
            for buf, ref, sem in (
                (out_buf, out_ref, out_sem),
                (dx_buf, dx_ref, dx_sem),
                (hid_buf, hid_ref, hid_sem),
                (dgu_buf, dgu_ref, dgu_sem),
            )
        ]

    c_copy(0).start()
    greet_neighbours(nz)
    own.wait()
    gather.row_step(0)
    for r in range(n_dp):
        w_load(r).wait()

    @pl.loop(0, steps)
    def _(m):
        @pl.when(m % 2 == 1)
        def _():
            n = (m + 1) // 2

            @pl.when(n < nz)
            def _():
                gather.row_step(n)

            gather.cross_step(n - 1)

        zs, yy = place(m)
        gather.ready(zs, yy)
        x_copy(m).start()

        @pl.when(m + 1 < steps)
        def _():
            c_copy(m + 1).start()

        @pl.when(m >= 2)
        def _():
            for copy in results(m - 2):
                copy.wait()

        c_copy(m).wait()
        s = m % 2
        x = g[zs, yy].reshape(pair_rows, g.shape[4])
        gate = dot_nn(x, w_ref[:, w_gate])
        up = dot_nn(x, w_ref[:, w_up])
        d_hid = dot_nn(c_buf[s], w_ref[:, w_down])
        sigma = 1.0 / (1.0 + jnp.exp(-gate))
        act = gate * sigma
        hid = (act * up).astype(BF16)
        d_gate = (d_hid * up * (sigma * (1.0 + gate * (1.0 - sigma)))).astype(BF16)
        d_up = (d_hid * act).astype(BF16)
        hid_buf[s] = hid
        dgu_buf[s, :, 0:hidden] = d_gate
        dgu_buf[s, :, hidden:] = d_up
        dx = dot_nt(d_gate, w_ref[:, w_gate]) + dot_nt(d_up, w_ref[:, w_up])
        dx_buf[s] = dx.astype(BF16)
        out_buf[s] = dot_nt(hid, w_ref[:, w_down]).astype(BF16)
        for copy in results(m):
            copy.start()

    for m in (steps - 2, steps - 1):
        for copy in results(m):
            copy.wait()

    @pl.loop(0, steps)
    def _(m):
        x_copy(m).wait()

    gather.drain()


def gather_mlp(xn, c_all, wm, wm_in, nz, n_dp):
    rows, width = xn.shape
    hidden = wm.shape[1] // 3
    pairs = nz * 2
    length = 2 * pairs * rows
    any_spec = pl.BlockSpec(memory_space=pl.ANY)
    dma = pltpu.SemaphoreType.DMA

    def by_pair(cols):
        return jax.ShapeDtypeStruct((pairs, 2 * rows, cols), BF16)

    def buffers(cols):
        return pltpu.VMEM((2, 2 * rows, cols), BF16)

    xn_all, out_part, dx_part, hid, d_gu = pl.pallas_call(
        functools.partial(gather_mlp_kernel, nz, n_dp),
        in_specs=[any_spec] * 4,
        out_specs=[any_spec] * 5,
        out_shape=[
            jax.ShapeDtypeStruct((nz, 2, 2, rows, width), BF16),
            by_pair(width),
            by_pair(width),
            by_pair(hidden),
            by_pair(2 * hidden),
        ],
        scratch_shapes=[
            pltpu.VMEM((nz, 2, 2, rows, width), BF16),
            pltpu.VMEM((width, 3 * hidden), BF16),
            buffers(width),
            buffers(width),
            buffers(width),
            buffers(hidden),
            buffers(2 * hidden),
            dma((n_dp,)),
            dma,
            dma((2,)),
            dma((pairs,)),
            dma((2,)),
            dma((2,)),
            dma((2,)),
            dma((2,)),
        ]
        + gather_sems(nz),
        compiler_params=pltpu.CompilerParams(
            vmem_limit_bytes=VMEM_LIMIT, collective_id=2, has_side_effects=True
        ),
        cost_estimate=pl.CostEstimate(
            flops=12 * length * width * hidden,
            bytes_accessed=60 * length * width,
            transcendentals=length * hidden,
        ),
        name="gather_mlp",
    )(xn, c_all.reshape(pairs, 2 * rows, width), wm, wm_in)
    return (
        xn_all.reshape(length, width),
        out_part.reshape(length, width),
        dx_part.reshape(length, width),
        hid.reshape(length, hidden),
        d_gu.reshape(length, 2 * hidden),
    )


def by_group(weight, groups, sections):
    rows, cols = weight.shape
    part = cols // (groups * sections)
    parts = weight.reshape(rows, sections, groups, part)
    return jnp.transpose(parts, (2, 0, 1, 3)).reshape(groups, rows, sections * part)


def body(tokens, block_order, gain_attn, w_qkv, w_out, gain_mlp, w_gate_up, w_down, cotangent):
    nz = lax.axis_size("hs")
    groups = nz * lax.axis_size("blk")
    n_dp = lax.axis_size("dp")
    tok_rows, width = tokens.shape
    shard = w_qkv.shape[0]
    length = groups * tok_rows

    order = block_order[0]
    slot_of_block = jnp.argsort(order).astype(jnp.int32)
    base, step = rope_tables(groups, tok_rows)

    gain_columns = jnp.pad(jnp.stack([gain_attn, gain_mlp], axis=1), ((0, 0), (0, 126)))
    wq_parts = jnp.concatenate(
        [
            by_group(w_qkv, groups, 3),
            jnp.broadcast_to(gain_columns[None], (groups,) + gain_columns.shape),
        ],
        axis=2,
    )
    xn1_all, qkv, gains, wqkv_mine, wmlp_mine, wout_full = gather_qkv(
        tokens, wq_parts, w_gate_up, w_down, w_out, nz, n_dp, 3 * width // groups
    )

    q, k, v, ctxt, lse, ctx_tok, cot_all, wmlp_other = attn_fwd(
        slot_of_block, order, qkv, base, step, cotangent, wmlp_mine, nz, n_dp, 512
    )

    x_float = tokens.astype(F32)
    gain_two = gains[1]
    y_mid = x_float + dot_nn(ctx_tok, wout_full)
    xn2 = rms_scale(y_mid, gain_two).astype(BF16)

    xn2_all, out_part, dx_part, hid, d_gu = gather_mlp(
        xn2, cot_all, wmlp_mine, wmlp_other, nz, n_dp
    )
    d_xn2, grad_mlp = scatter_mlp(dx_part, xn2_all, cot_all, d_gu, hid, nz, 3)
    _, pull_two = jax.vjp(lambda v: rms_scale(v, gain_two), y_mid)
    (dy_norm,) = pull_two(d_xn2)
    d_mid = cotangent.astype(F32) + dy_norm
    d_mid_b = d_mid.astype(BF16)

    d_ctx = dot_nt(d_mid_b, wout_full).astype(BF16)
    grad_out = dot_tn(ctx_tok, d_mid_b).astype(BF16).reshape(n_dp, nz, 2, 2, shard, width)
    grad_mlp = grad_mlp.reshape(n_dp, groups, shard, -1)

    d_qkv, mlp_out, grad_out_in, grad_qkv, mlp_early = attn_bwd(
        slot_of_block, order, q, k, v, d_ctx, ctxt, lse, base, step, out_part, grad_out, xn1_all,
        grad_mlp, nz, 512,
    )
    sums, grad_qkv, mlp_late = scatter_last(
        d_qkv, wqkv_mine, grad_qkv, grad_mlp, grad_out, grad_out_in, nz, n_dp, 4
    )
    (
        qkv_rows, gu_rows, down_rows, grad_gain_one, grad_gain_two, layer_out, grad_tokens, out_rows,
    ) = layout_call(
        grad_qkv, mlp_early, mlp_late, w_qkv, w_gate_up, gain_attn, gain_mlp,
        sums, tokens, gains, d_mid, y_mid, mlp_out,
    )
    return (
        layer_out,
        grad_tokens,
        grad_gain_one.reshape(shard),
        qkv_rows,
        out_rows,
        grad_gain_two.reshape(shard),
        gu_rows,
        down_rows,
    )


def solution(mesh):
    rows = P(ALL, None)
    in_specs = (rows, P("dp", None), P(ALL), rows, rows, P(ALL), rows, rows, rows)
    out_specs = (rows, rows, P(ALL), rows, rows, P(ALL), rows, rows)
    return jax.shard_map(body, mesh=mesh, in_specs=in_specs, out_specs=out_specs, check_vma=False)
```
